32 devices in a mesh: gx: 4 (over z), gy: 4 (over y, core), gz: 2 (over x).
Axes of the slice: x: 2, y: 2, z: 4, core: 2. Of those that a mesh axis runs over, the one named last changes fastest.
Arguments:
- incident: bfloat16 [4, 4, 2, 2, 1280, 128], P('gx', 'gy', 'gz'), may hold values from -6 to 6
- response: bfloat16 [4, 4, 2, 2, 1280, 1280], P('gx', 'gy', 'gz'), may hold values from -0.125 to 0.125
- radiation: bfloat16 [4, 4, 2, 2, 512, 1280], P('gx', 'gy', 'gz'), may hold values from -0.01953125 to 0.01953125
- face_index: int32 [4, 4, 2, 6, 192], P('gx', 'gy', 'gz'), may hold values from 0 to 1279, as said below
- linked: int32 [4, 4, 2, 6], P('gx', 'gy', 'gz'), may hold values 0 or 1
Outputs:
- far_field: float32 [2, 128, 512], P(None, ('gx', 'gy'), 'gz')
The draws below stay inside these ranges and needn't reach their ends.
Inputs may be any that keep to these rules, and one draw needn't show every extreme that they name: `face_index`: the 1152 entries of one subdomain are distinct.
All inputs are finite; a program needn't handle non-finite values. No bound on the sum of `linked` on one device may be relied on, other than what follows from the above.
Results may differ from the reference program's by a relative error of at most 0.004.
Values may be sent and summed in bfloat16 or wider, within the bound.
No kernel may reach another device: no remote copies, remote signals or barrier semaphores. Data moves between devices by JAX's collectives and lax.ppermute only.
A program may use at most 64 MiB of HBM per device.

```python
import jax
import jax.numpy as jnp
from jax import lax

M = 1280
FACE = 192
ANG = 512
EXC = 128
ITERS = 2
N_GX = 4
N_GY = 4
N_GZ = 2


def draw_face_index(key, part):
    keys = jax.random.split(jax.random.fold_in(key, 17), N_GX * N_GY * N_GZ)
    picks = jax.vmap(lambda single: jax.random.permutation(single, M)[:6 * FACE])(keys)
    return picks.reshape(N_GX, N_GY, N_GZ, 6, FACE).astype(jnp.int32)


def with_ends(result, rng, low, high):
    longest = result.shape.index(max(result.shape))
    spots = []
    for shift in (0, 1):
        where = [jax.random.randint(jax.random.fold_in(rng, axis), (), 0, length) for axis, length in enumerate(result.shape)]
        where[longest] = (where[longest] + shift) % result.shape[longest]
        spots.append(tuple(where))
    return result.at[spots[0]].set(low).at[spots[1]].set(high)


def level_of(key, dims, cuts, least, top_value):
    loudness = 1.0
    for dim, shards_of in cuts:
        heights = jax.random.uniform(jax.random.fold_in(jax.random.fold_in(key, 6), dim), (shards_of,), jnp.float32, least / len(cuts), top_value / len(cuts))
        loudness = loudness * jnp.repeat(jnp.exp(heights), dims[dim] // shards_of).reshape((-1,) + (1,) * (len(dims) - 1 - dim))
    return loudness


def gaussian(stream_key, dims, scale, most, shards=(), kind=jnp.bfloat16):
    array = scale * jax.random.normal(stream_key, dims, jnp.float32)
    if shards:
        array = array * level_of(stream_key, dims, shards, -0.22, 0.18)
    return jnp.clip(array, -most, most).astype(kind)


def setup_inputs(seed: int = 0) -> dict:
    arg_keys = jax.random.split(jax.random.key(seed), 6)
    incident = gaussian(arg_keys[0], (N_GX, N_GY, N_GZ, 2, M, EXC), 1.0, 6.0, ((0, 4), (1, 4), (2, 2)))
    response = gaussian(arg_keys[1], (N_GX, N_GY, N_GZ, 2, M, M), (2 * M) ** -0.5, 0.125, ((0, 4), (1, 4), (2, 2)))
    radiation = gaussian(arg_keys[2], (N_GX, N_GY, N_GZ, 2, ANG, M), (2 * M * N_GX * N_GY * N_GZ) ** -0.5, 0.01953125, ((0, 4), (1, 4), (2, 2)))
    face_index = draw_face_index(jax.random.fold_in(arg_keys[5], 71), 0)
    linked = with_ends((jax.random.randint(arg_keys[4], (N_GX, N_GY, N_GZ, 6), 0, 4) < 3).astype(jnp.int32), jax.random.fold_in(arg_keys[4], 1), 0, 1)
    return dict(incident=incident, response=response, radiation=radiation, face_index=face_index, linked=linked)


def complex_dot(left_side, right_side):
    real_part = jnp.dot(left_side[0], right_side[0], preferred_element_type=jnp.float32) - jnp.dot(left_side[1], right_side[1], preferred_element_type=jnp.float32)
    imag_part = jnp.dot(left_side[0], right_side[1], preferred_element_type=jnp.float32) + jnp.dot(left_side[1], right_side[0], preferred_element_type=jnp.float32)
    return jnp.stack([real_part, imag_part])


def from_lower(values, dim):
    blank = jnp.zeros_like(lax.slice_in_dim(values, 0, 1, axis=dim))
    return jnp.concatenate([blank, lax.slice_in_dim(values, 0, values.shape[dim] - 1, axis=dim)], dim)


def from_upper(values, dim):
    blank = jnp.zeros_like(lax.slice_in_dim(values, 0, 1, axis=dim))
    return jnp.concatenate([lax.slice_in_dim(values, 1, values.shape[dim], axis=dim), blank], dim)


def place_rows(slots, values):
    blank = jnp.zeros((2, M, values.shape[-1]), values.dtype)
    return blank.at[:, slots].set(values.reshape(2, 6 * FACE, values.shape[-1]))


def reference(incident, response, radiation, face_index, linked):
    count = N_GX * N_GY * N_GZ
    flat_incident = incident.reshape(count, 2, M, EXC)
    flat_response = response.reshape(count, 2, M, M)
    flat_radiation = radiation.reshape(count, 2, ANG, M)
    flat_slots = face_index.reshape(count, 6 * FACE).astype(jnp.int32)
    flat_linked = linked.reshape(count, 6)
    traces = jnp.zeros((count, 2, M, EXC), incident.dtype)
    for sweep in range(ITERS):
        summed = (traces.astype(jnp.float32) + flat_incident.astype(jnp.float32)).astype(jnp.bfloat16)
        outgoing = lax.map(lambda pair: complex_dot(pair[0], pair[1]).astype(jnp.bfloat16), (flat_response, summed))
        faces = jax.vmap(lambda rows, slots: rows[:, slots, :])(outgoing, flat_slots)
        faces = faces.reshape(N_GX, N_GY, N_GZ, 2, 6, FACE, EXC)
        arrived = []
        for axis_pos in range(3):
            arrived.append(from_lower(faces[:, :, :, :, 2 * axis_pos + 1], axis_pos))
            arrived.append(from_upper(faces[:, :, :, :, 2 * axis_pos], axis_pos))
        incoming = jnp.stack(arrived, 4).reshape(count, 2, 6, FACE, EXC)
        incoming = incoming * flat_linked[:, None, :, None, None].astype(incoming.dtype)
        traces = jax.vmap(place_rows)(flat_slots, incoming)
    currents = (traces.astype(jnp.float32) + flat_incident.astype(jnp.float32)).astype(jnp.bfloat16)

    def accumulate(total, pair):
        return total + complex_dot(pair[0], pair[1]), None

    total, unused = lax.scan(accumulate, jnp.zeros((2, ANG, EXC), jnp.float32), (flat_radiation, currents))
    return jnp.transpose(total, (0, 2, 1))
```

```python
import functools

import jax
import jax.numpy as jnp
from jax import lax
from jax.experimental import pallas as pl
from jax.experimental.pallas import tpu as pltpu
from jax.sharding import PartitionSpec as P

ITERS = 2
AXES = ("gx", "gy", "gz")
F32 = jnp.float32
BF16 = jnp.bfloat16
CHUNKS = 5
VMEM_LIMIT = 40 * 1024 * 1024


def swap_rounds(sizes):
    rounds = []
    for pos, size in enumerate(sizes):
        if size > 1:
            rounds.append((pos, 0))
        if size > 2:
            rounds.append((pos, 1))
    return rounds


def swap_pairs(size, phase):
    pairs = []
    for low in range(phase, size - 1, 2):
        pairs += [(low, low + 1), (low + 1, low)]
    return pairs


def chosen_rows(slots_ref, ids_ref, count):
    return [slots_ref[pl.ds(ids_ref[pos], 1), :] for pos in range(count)]


def put_traces(rows, arrived, linked_ref, ids_ref, unknowns, width):
    total = None
    for pos, row in enumerate(rows):
        face = row.shape[-1]
        spots = lax.broadcasted_iota(jnp.int32, (unknowns, face), 0)
        chosen = jnp.where(spots == row, 1.0, 0.0).astype(BF16)
        gate = linked_ref[ids_ref[pos]].astype(F32)
        values = (arrived[pos][...].astype(F32) * gate).astype(BF16)
        part = jnp.dot(chosen, values, preferred_element_type=F32)
        total = part if total is None else total + part
    return total


def join(left, right):
    return jnp.concatenate([left, right], axis=1)


def sweep_kernel(count, first, ids_ref, linked_ref, slots_hbm, source_hbm, response_hbm, *refs):
    arrived = () if first else refs[:count]
    outs = refs[len(arrived) : len(arrived) + count]
    slots, source, response, straight, crossed, outgoing, sems = refs[len(arrived) + count :]
    unknowns = source.shape[1]
    columns = source.shape[2]
    step = unknowns // CHUNKS
    small = [
        pltpu.make_async_copy(slots_hbm, slots, sems.at[0]),
        pltpu.make_async_copy(source_hbm, source, sems.at[1]),
    ]
    large = [
        pltpu.make_async_copy(
            response_hbm.at[:, pl.ds(pos * step, step), :],
            response.at[:, pl.ds(pos * step, step), :],
            sems.at[2 + pos],
        )
        for pos in range(CHUNKS)
    ]
    for copy in small + large:
        copy.start()
    for copy in small:
        copy.wait()
    rows = chosen_rows(slots, ids_ref, count)
    if first:
        real, imag = source[0], source[1]
    else:
        traces = put_traces(rows, arrived, linked_ref, ids_ref, unknowns, 2 * columns)
        real = (traces[:, :columns] + source[0].astype(F32)).astype(BF16)
        imag = (traces[:, columns:] + source[1].astype(F32)).astype(BF16)
    straight[...] = join(real, imag)
    crossed[...] = join(-imag, real)
    for pos in range(CHUNKS):
        large[pos].wait()
        part = pl.ds(pos * step, step)
        outgoing[part, :] = (
            jnp.dot(response[0, part, :], straight[...], preferred_element_type=F32)
            + jnp.dot(response[1, part, :], crossed[...], preferred_element_type=F32)
        ).astype(BF16)
    face = slots.shape[1]
    padded = jnp.concatenate(rows + [rows[0]] * (8 - count), axis=0)
    upright = jnp.transpose(padded)
    spots = lax.broadcasted_iota(jnp.int32, (face, unknowns), 1)
    for pos in range(count):
        chosen = jnp.where(spots == upright[:, pos : pos + 1], 1.0, 0.0).astype(BF16)
        outs[pos][...] = jnp.dot(chosen, outgoing[...], preferred_element_type=F32).astype(BF16)


def radiate_kernel(count, ids_ref, linked_ref, slots_hbm, source_hbm, radiation_hbm, *refs):
    arrived = refs[:count]
    out = refs[count]
    slots, source, radiation, sems = refs[count + 1 :]
    unknowns = source.shape[1]
    columns = source.shape[2]
    copies = [
        pltpu.make_async_copy(slots_hbm, slots, sems.at[0]),
        pltpu.make_async_copy(source_hbm, source, sems.at[1]),
        pltpu.make_async_copy(radiation_hbm, radiation, sems.at[2]),
    ]
    for copy in copies:
        copy.start()
    for copy in copies[:2]:
        copy.wait()
    rows = chosen_rows(slots, ids_ref, count)
    traces = put_traces(rows, arrived, linked_ref, ids_ref, unknowns, 2 * columns)
    real = (traces[:, :columns] + source[0].astype(F32)).astype(BF16)
    imag = (traces[:, columns:] + source[1].astype(F32)).astype(BF16)
    straight = join(real, imag)
    crossed = join(-imag, real)
    copies[2].wait()
    field = jnp.dot(radiation[0], straight, preferred_element_type=F32) + jnp.dot(
        radiation[1], crossed, preferred_element_type=F32
    )
    out[0] = jnp.transpose(field[:, :columns])
    out[1] = jnp.transpose(field[:, columns:])


def any_spec():
    return pl.BlockSpec(memory_space=pl.ANY)


def smem_spec():
    return pl.BlockSpec(memory_space=pltpu.SMEM)


def vmem_spec():
    return pl.BlockSpec(memory_space=pltpu.VMEM)


def sweep(ids, linked, slots, source, response, arrived, count):
    unknowns, columns = source.shape[1:]
    face = slots.shape[1]
    first = arrived is None
    got = () if first else tuple(arrived)
    return pl.pallas_call(
        functools.partial(sweep_kernel, count, first),
        out_shape=[jax.ShapeDtypeStruct((face, 2 * columns), BF16)] * count,
        in_specs=[smem_spec(), smem_spec(), any_spec(), any_spec(), any_spec()] + [vmem_spec()] * len(got),
        out_specs=[vmem_spec()] * count,
        scratch_shapes=[
            pltpu.VMEM(slots.shape, slots.dtype),
            pltpu.VMEM(source.shape, BF16),
            pltpu.VMEM(response.shape, BF16),
            pltpu.VMEM((unknowns, 2 * columns), BF16),
            pltpu.VMEM((unknowns, 2 * columns), BF16),
            pltpu.VMEM((unknowns, 2 * columns), BF16),
            pltpu.SemaphoreType.DMA((2 + CHUNKS,)),
        ],
        compiler_params=pltpu.CompilerParams(vmem_limit_bytes=VMEM_LIMIT),
    )(ids, linked, slots, source, response, *got)


def radiate(ids, linked, slots, source, radiation, arrived, count):
    columns = source.shape[2]
    angles = radiation.shape[1]
    return pl.pallas_call(
        functools.partial(radiate_kernel, count),
        out_shape=jax.ShapeDtypeStruct((2, columns, angles), F32),
        in_specs=[smem_spec(), smem_spec(), any_spec(), any_spec(), any_spec()] + [vmem_spec()] * count,
        out_specs=vmem_spec(),
        scratch_shapes=[
            pltpu.VMEM(slots.shape, slots.dtype),
            pltpu.VMEM(source.shape, BF16),
            pltpu.VMEM(radiation.shape, BF16),
            pltpu.SemaphoreType.DMA((3,)),
        ],
        compiler_params=pltpu.CompilerParams(vmem_limit_bytes=VMEM_LIMIT),
    )(ids, linked, slots, source, radiation, *arrived)


def bit_count(size):
    return size.bit_length() - 1


def mask_pairs(sizes, flips):
    pairs = []
    for at_x in range(sizes[0]):
        for at_y in range(sizes[1]):
            for at_z in range(sizes[2]):
                here = (at_x * sizes[1] + at_y) * sizes[2] + at_z
                there = ((at_x ^ flips[0]) * sizes[1] + (at_y ^ flips[1])) * sizes[2] + (at_z ^ flips[2])
                pairs.append((here, there))
    return pairs


def scatter_sum(field, sizes, where):
    columns, angles = field.shape[1:]
    bits = [bit_count(size) for size in sizes]
    dims = {}
    shape = [2]
    for pos in (0, 1):
        for bit in reversed(range(bits[pos])):
            dims[(pos, bit)] = len(shape)
            shape.append(2)
    shape.append(columns // (sizes[0] * sizes[1]))
    for bit in reversed(range(bits[2])):
        dims[(2, bit)] = len(shape)
        shape.append(2)
    shape.append(angles // sizes[2])
    rounds = []
    rest = [(pos, bit) for bit in range(max(bits)) for pos in (1, 2, 0) if bit < bits[pos]]
    if (1, 0) in rest:
        rest.remove((1, 0))
        rounds.append([(1, 0)])
    planes = [item for item in rest if item[0] != 0] + [item for item in rest if item[0] == 0]
    rounds += [planes[pos : pos + 2] for pos in range(0, len(planes), 2)]
    total = field.reshape(shape)
    for group in rounds:
        def taken(code):
            piece = total
            for order, (pos, bit) in enumerate(group):
                mine = (where[pos] >> bit) & 1
                piece = lax.dynamic_slice_in_dim(piece, mine ^ ((code >> order) & 1), 1, axis=dims[(pos, bit)])
            return piece

        got = []
        for code in range(1, 2 ** len(group)):
            flips = [0, 0, 0]
            for order, (pos, bit) in enumerate(group):
                flips[pos] |= ((code >> order) & 1) << bit
            got.append(lax.ppermute(taken(code).astype(BF16), AXES, mask_pairs(sizes, flips)))
        total = taken(0)
        for piece in got:
            total = total + piece.astype(F32)
    return total.reshape(2, columns // (sizes[0] * sizes[1]), angles // sizes[2])


def shards(sizes, incident, response, radiation, face_index, linked):
    source = incident[0, 0, 0]
    response_mat = response[0, 0, 0]
    radiation_mat = radiation[0, 0, 0]
    slots = face_index[0, 0, 0]
    linked_faces = linked[0, 0, 0]
    where = [lax.axis_index(axis) for axis in AXES]
    rounds = swap_rounds(sizes)
    count = len(rounds)
    ids = jnp.stack([2 * pos + 1 - ((where[pos] + phase) & 1) for pos, phase in rounds]).astype(jnp.int32)
    arrived = None
    for turn in range(ITERS):
        faces = sweep(ids, linked_faces, slots, source, response_mat, arrived, count)
        arrived = [
            lax.ppermute(face, AXES[pos], swap_pairs(sizes[pos], phase))
            for face, (pos, phase) in zip(faces, rounds)
        ]
    field = radiate(ids, linked_faces, slots, source, radiation_mat, arrived, count)
    return scatter_sum(field, sizes, where)


def solution(mesh):
    sizes = tuple(mesh.shape[axis] for axis in AXES)
    return jax.shard_map(
        functools.partial(shards, sizes),
        mesh=mesh,
        in_specs=(
            P("gx", "gy", "gz", None, None, None),
            P("gx", "gy", "gz", None, None, None),
            P("gx", "gy", "gz", None, None, None),
            P("gx", "gy", "gz", None, None),
            P("gx", "gy", "gz", None),
        ),
        out_specs=P(None, ("gx", "gy"), "gz"),
        check_vma=False,
    )
```

```python
import functools

import jax
import jax.numpy as jnp
from jax import lax
from jax.experimental import pallas as pl
from jax.experimental.pallas import tpu as pltpu
from jax.sharding import PartitionSpec as P

ITERS = 2
AXES = ("gx", "gy", "gz")
F32 = jnp.float32
BF16 = jnp.bfloat16
CHUNKS = 5
VMEM_LIMIT = 40 * 1024 * 1024
OUT_VMEM = pltpu.VMEM


def swap_rounds(sizes):
    rounds = []
    for pos, size in enumerate(sizes):
        if size > 1:
            rounds.append((pos, 0))
        if size > 2:
            rounds.append((pos, 1))
    return rounds


def partner_of(sizes, pos, phase, here):
    there = list(here)
    near = here[pos] + (1 if (here[pos] + phase) % 2 == 0 else -1)
    if 0 <= near < sizes[pos]:
        there[pos] = near
    elif pos == 1 or sizes[1] % 2:
        there[pos] = sizes[pos] - 1 - here[pos]
    else:
        there[1] = here[1] ^ 1
    return there


def swap_pairs(sizes, pos, phase):
    pairs = []
    for at_x in range(sizes[0]):
        for at_y in range(sizes[1]):
            for at_z in range(sizes[2]):
                there = partner_of(sizes, pos, phase, (at_x, at_y, at_z))
                if there != [at_x, at_y, at_z]:
                    pairs.append(
                        ((at_x * sizes[1] + at_y) * sizes[2] + at_z, (there[0] * sizes[1] + there[1]) * sizes[2] + there[2])
                    )
    return pairs


def has_neighbour(sizes, where, pos, phase):
    near = where[pos] + 1 - 2 * ((where[pos] + phase) & 1)
    return jnp.logical_and(near >= 0, near < sizes[pos])


def face_id(where, pos, phase):
    return 2 * pos + 1 - ((where[pos] + phase) & 1)


def join(left, right):
    return jnp.concatenate([left, right], axis=1)


def blocks(total):
    return [pl.ds(pos * (total // CHUNKS), total // CHUNKS) for pos in range(CHUNKS)]


def respond(response, straight, crossed, outgoing, part):
    outgoing[part, :] = (
        jnp.dot(response[0, part, :], straight[...], preferred_element_type=F32)
        + jnp.dot(response[1, part, :], crossed[...], preferred_element_type=F32)
    ).astype(BF16)


def pick_faces(picks, outgoing, outs):
    face = outs[0].shape[0]
    chosen = jnp.dot(picks[...], outgoing[...], preferred_element_type=F32).astype(BF16)
    for pos, out in enumerate(outs):
        out[...] = chosen[pos * face : (pos + 1) * face]


def add_traces(puts, arrived, source, values, part):
    traces = jnp.dot(puts[part, :], values[...], preferred_element_type=F32)
    return (traces + source[part, :].astype(F32)).astype(BF16)


def gather_values(arrived, values):
    face = arrived[0].shape[0]
    for pos, faces in enumerate(arrived):
        values[pl.ds(pos * face, face), :] = faces[...]


def turned(both):
    columns = both.shape[1] // 2
    return join(-both[:, columns:], both[:, :columns])


def first_kernel(sizes, rounds, linked_hbm, slots_hbm, source_hbm, response_hbm, *refs):
    count = len(rounds)
    outs = refs[:count]
    response, source, puts, picks = refs[count : count + 4]
    linked, slots, parts, crossed, outgoing, sems = refs[count + 4 :]
    unknowns, face = response.shape[1], slots.shape[2]
    small = [
        pltpu.make_async_copy(linked_hbm, linked, sems.at[0]),
        pltpu.make_async_copy(slots_hbm, slots, sems.at[1]),
        pltpu.make_async_copy(source_hbm, parts, sems.at[2]),
    ]
    large = [
        pltpu.make_async_copy(response_hbm.at[:, part, :], response.at[:, part, :], sems.at[3 + pos])
        for pos, part in enumerate(blocks(unknowns))
    ]
    for copy in small + large:
        copy.start()
    for copy in small:
        copy.wait()
    where = [lax.axis_index(axis) for axis in AXES]
    ids = [face_id(where, pos, phase) for pos, phase in rounds]
    rows = [slots[face_pos] for face_pos in ids]
    source[...] = join(parts[0], parts[1])
    crossed[...] = turned(source)
    upright = jnp.transpose(jnp.concatenate(rows + [rows[0]] * (-count % 8), axis=0))
    gates = [
        jnp.logical_and(linked[face_pos] != 0, has_neighbour(sizes, where, pos, phase))
        for face_pos, (pos, phase) in zip(ids, rounds)
    ]
    accepted = jnp.concatenate([jnp.where(gate, row, -1) for gate, row in zip(gates, rows)], axis=1)
    across = lax.broadcasted_iota(jnp.int32, (face, unknowns), 1)
    parts_of = blocks(unknowns)
    for step in range(max(count, CHUNKS)):
        if step < count:
            chosen = jnp.where(across == upright[:, step : step + 1], 1.0, 0.0)
            picks[pl.ds(step * face, face), :] = chosen.astype(BF16)
        if step < CHUNKS:
            part = parts_of[step]
            down = part.start + lax.broadcasted_iota(jnp.int32, (part.size, count * face), 0)
            puts[part, :] = jnp.where(down == accepted, 1.0, 0.0).astype(BF16)
            large[step].wait()
            respond(response, source, crossed, outgoing, part)
    pick_faces(picks, outgoing, outs)


def sweep_kernel(count, response, source, puts, picks, *refs):
    arrived, outs = refs[:count], refs[count : 2 * count]
    values, straight, crossed, outgoing = refs[2 * count :]
    gather_values(arrived, values)
    for part in blocks(source.shape[0]):
        both = add_traces(puts, arrived, source, values, part)
        straight[part, :] = both
        crossed[part, :] = turned(both)
    for part in blocks(source.shape[0]):
        respond(response, straight, crossed, outgoing, part)
    pick_faces(picks, outgoing, outs)


def radiate_kernel(count, halves, eb, source, puts, radiation, *refs):
    arrived, outs = refs[:count], refs[count : count + 1 + halves]
    values, straight, crossed = refs[count + 1 + halves :]
    columns = source.shape[1] // 2
    gather_values(arrived, values)
    for part in blocks(source.shape[0]):
        both = add_traces(puts, arrived, source, values, part)
        straight[part, :] = both
        crossed[part, :] = turned(both)
    field = jnp.dot(radiation[0], straight[...], preferred_element_type=F32) + jnp.dot(
        radiation[1], crossed[...], preferred_element_type=F32
    )
    mine = lax.axis_index("gy") & 1
    for part in range(2):
        flat = jnp.transpose(field[:, part * columns : (part + 1) * columns])
        if not halves:
            outs[0][part] = flat
            continue
        split = [
            jnp.concatenate([flat[low : low + eb] for low in range(half * eb, columns, 2 * eb)], axis=0)
            for half in range(2)
        ]
        outs[0][part] = jnp.where(mine == 0, split[0], split[1])
        outs[1][part] = jnp.where(mine == 0, split[1], split[0])


def hbm_spec():
    return pl.BlockSpec(memory_space=pl.ANY)


def vmem_spec():
    return pl.BlockSpec(memory_space=pltpu.VMEM)


def in_hbm(value):
    return pltpu.with_memory_space_constraint(value, pltpu.HBM)


def in_vmem(value):
    return pltpu.with_memory_space_constraint(value, pltpu.VMEM)


def params():
    return pltpu.CompilerParams(vmem_limit_bytes=VMEM_LIMIT)


def first_sweep(sizes, rounds, linked, slots, source, response):
    unknowns, columns = source.shape[1:]
    face, count = slots.shape[2], len(rounds)
    kept = [
        (response.shape, BF16),
        ((unknowns, 2 * columns), BF16),
        ((unknowns, count * face), BF16),
        ((count * face, unknowns), BF16),
    ]
    outs = pl.pallas_call(
        functools.partial(first_kernel, sizes, rounds),
        out_shape=[jax.ShapeDtypeStruct((face, 2 * columns), BF16)] * count
        + [OUT_VMEM(shape, kind) for shape, kind in kept],
        in_specs=[hbm_spec()] * 4,
        out_specs=[vmem_spec()] * (count + len(kept)),
        scratch_shapes=[
            pltpu.SMEM(linked.shape, linked.dtype),
            pltpu.VMEM(slots.shape, slots.dtype),
            pltpu.VMEM(source.shape, BF16),
            pltpu.VMEM((unknowns, 2 * columns), BF16),
            pltpu.VMEM((unknowns, 2 * columns), BF16),
            pltpu.SemaphoreType.DMA((3 + CHUNKS,)),
        ],
        compiler_params=params(),
    )(in_hbm(linked), in_hbm(slots), in_hbm(source), in_hbm(response))
    return outs[:count], outs[count:]


def later_sweep(kept, arrived):
    response, source, puts, picks = kept
    count = len(arrived)
    return pl.pallas_call(
        functools.partial(sweep_kernel, count),
        out_shape=[jax.ShapeDtypeStruct(arrived[0].shape, BF16)] * count,
        in_specs=[vmem_spec()] * (4 + count),
        out_specs=[vmem_spec()] * count,
        scratch_shapes=[pltpu.VMEM((picks.shape[0], source.shape[1]), BF16)]
        + [pltpu.VMEM(source.shape, BF16)] * 3,
        compiler_params=params(),
    )(response, source, puts, picks, *arrived)


def radiate(kept, radiation, arrived, halves, eb):
    source, puts, picks = kept[1:]
    columns = source.shape[1] // 2
    angles = radiation.shape[1]
    count = len(arrived)
    shape = (2, columns // 2 if halves else columns, angles)
    outs = [jax.ShapeDtypeStruct(shape, F32)] * (1 + int(halves))
    return pl.pallas_call(
        functools.partial(radiate_kernel, count, int(halves), eb),
        out_shape=outs,
        in_specs=[vmem_spec()] * (3 + count),
        out_specs=[vmem_spec()] * len(outs),
        scratch_shapes=[pltpu.VMEM((picks.shape[0], source.shape[1]), BF16)]
        + [pltpu.VMEM(source.shape, BF16)] * 2,
        compiler_params=params(),
    )(source, puts, radiation, *arrived)


def bit_count(size):
    return size.bit_length() - 1


def mask_pairs(sizes, flips):
    pairs = []
    for at_x in range(sizes[0]):
        for at_y in range(sizes[1]):
            for at_z in range(sizes[2]):
                here = (at_x * sizes[1] + at_y) * sizes[2] + at_z
                there = ((at_x ^ flips[0]) * sizes[1] + (at_y ^ flips[1])) * sizes[2] + (at_z ^ flips[2])
                pairs.append((here, there))
    return pairs


def scatter_sum(parts, sizes, where, full):
    columns, angles = full
    bits = [bit_count(size) for size in sizes]
    halves = len(parts) > 1
    dims = {}
    shape = [2]
    for pos in (0, 1):
        for bit in reversed(range(bits[pos])):
            if halves and (pos, bit) == (1, 0):
                continue
            dims[(pos, bit)] = len(shape)
            shape.append(2)
    shape.append(columns // (sizes[0] * sizes[1]))
    for bit in reversed(range(bits[2])):
        dims[(2, bit)] = len(shape)
        shape.append(2)
    shape.append(angles // sizes[2])
    total = parts[0]
    if halves:
        total = total + lax.ppermute(parts[1], AXES, mask_pairs(sizes, (0, 1, 0)))
    total = total.reshape(shape)
    rest = [item for item in dims if item[0] != 0]
    rest = sorted(rest, key=lambda item: (item[1], item[0])) + sorted(item for item in dims if item[0] == 0)
    rounds = [rest[pos : pos + 2] for pos in range(0, len(rest), 2)]
    for order, group in enumerate(rounds):
        wide = order == len(rounds) - 1

        def taken(code):
            piece = total
            for place, (pos, bit) in enumerate(group):
                mine = (where[pos] >> bit) & 1
                piece = lax.dynamic_slice_in_dim(piece, mine ^ ((code >> place) & 1), 1, axis=dims[(pos, bit)])
            return piece

        got = []
        for code in range(1, 2 ** len(group)):
            flips = [0, 0, 0]
            for place, (pos, bit) in enumerate(group):
                flips[pos] |= ((code >> place) & 1) << bit
            piece = taken(code) if wide else taken(code).astype(BF16)
            got.append(lax.ppermute(piece, AXES, mask_pairs(sizes, flips)))
        total = taken(0)
        for piece in got:
            total = total + piece.astype(F32)
    return total.reshape(2, columns // (sizes[0] * sizes[1]), angles // sizes[2])


def shards(sizes, incident, response, radiation, face_index, linked):
    source = incident[0, 0, 0]
    response_mat = response[0, 0, 0]
    radiation_mat = radiation[0, 0, 0]
    slots = face_index[0, 0, 0][:, None, :]
    where = [lax.axis_index(axis) for axis in AXES]
    rounds = swap_rounds(sizes)
    columns, angles = source.shape[2], radiation_mat.shape[1]
    faces, kept = first_sweep(sizes, rounds, linked[0, 0, 0], slots, source, response_mat)
    for turn in range(ITERS):
        arrived = [
            lax.ppermute(face, AXES, swap_pairs(sizes, pos, phase))
            for face, (pos, phase) in zip(faces, rounds)
        ]
        if turn < ITERS - 1:
            faces = later_sweep(kept, arrived)
    halves = sizes[1] % 2 == 0
    parts = radiate(kept, radiation_mat, arrived, halves, columns // (sizes[0] * sizes[1]))
    return scatter_sum(parts, sizes, where, (columns, angles))


def solution(mesh):
    sizes = tuple(mesh.shape[axis] for axis in AXES)
    return jax.shard_map(
        functools.partial(shards, sizes),
        mesh=mesh,
        in_specs=(
            P("gx", "gy", "gz", None, None, None),
            P("gx", "gy", "gz", None, None, None),
            P("gx", "gy", "gz", None, None, None),
            P("gx", "gy", "gz", None, None),
            P("gx", "gy", "gz", None),
        ),
        out_specs=P(None, ("gx", "gy"), "gz"),
        check_vma=False,
    )
```

```python
import functools

import jax
import jax.numpy as jnp
from jax import lax
from jax.experimental import pallas as pl
from jax.experimental.pallas import tpu as pltpu
from jax.sharding import PartitionSpec as P

ITERS = 2
AXES = ("gx", "gy", "gz")
F32 = jnp.float32
BF16 = jnp.bfloat16
CHUNKS = 8
STAGES = (4, 6, 8)
VMEM_LIMIT = 40 * 1024 * 1024
OUT_VMEM = pltpu.VMEM


def swap_rounds(sizes):
    rounds = [(pos, phase) for pos in (0, 2) for phase in (0, 1)] + [(1, 1), (1, 0)]
    return [(pos, phase) for pos, phase in rounds if sizes[pos] > 1 + phase]


def partner_of(sizes, pos, phase, here):
    there = list(here)
    near = here[pos] + (1 if (here[pos] + phase) % 2 == 0 else -1)
    if 0 <= near < sizes[pos]:
        there[pos] = near
    elif pos == 1 or sizes[1] % 2:
        there[pos] = sizes[pos] - 1 - here[pos]
    else:
        there[1] = here[1] ^ 1
    return there


def swap_pairs(sizes, pos, phase):
    pairs = []
    for at_x in range(sizes[0]):
        for at_y in range(sizes[1]):
            for at_z in range(sizes[2]):
                there = partner_of(sizes, pos, phase, (at_x, at_y, at_z))
                if there != [at_x, at_y, at_z]:
                    pairs.append(
                        ((at_x * sizes[1] + at_y) * sizes[2] + at_z, (there[0] * sizes[1] + there[1]) * sizes[2] + there[2])
                    )
    return pairs


def has_neighbour(sizes, where, pos, phase):
    near = where[pos] + 1 - 2 * ((where[pos] + phase) & 1)
    return jnp.logical_and(near >= 0, near < sizes[pos])


def face_id(where, pos, phase):
    return 2 * pos + 1 - ((where[pos] + phase) & 1)


def join(left, right):
    return jnp.concatenate([left, right], axis=1)


def blocks(total):
    return [pl.ds(pos * (total // CHUNKS), total // CHUNKS) for pos in range(CHUNKS)]


def respond(response, straight, crossed, outgoing, part):
    outgoing[part, :] = (
        jnp.dot(response[0, part, :], straight[...], preferred_element_type=F32)
        + jnp.dot(response[1, part, :], crossed[...], preferred_element_type=F32)
    ).astype(BF16)


def pick_faces(picks, outgoing, outs):
    face = outs[0].shape[0]
    chosen = jnp.dot(picks[...], outgoing[...], preferred_element_type=F32).astype(BF16)
    for pos, out in enumerate(outs):
        out[...] = chosen[pos * face : (pos + 1) * face]


def add_traces(puts, arrived, source, values, part):
    traces = jnp.dot(puts[part, :], values[...], preferred_element_type=F32)
    return (traces + source[part, :].astype(F32)).astype(BF16)


def gather_values(arrived, values):
    face = arrived[0].shape[0]
    for pos, faces in enumerate(arrived):
        values[pl.ds(pos * face, face), :] = faces[...]


def turned(both):
    columns = both.shape[1] // 2
    return join(-both[:, columns:], both[:, :columns])


def first_kernel(sizes, rounds, linked_hbm, slots_hbm, source_hbm, response_hbm, *refs):
    count = len(rounds)
    outs = refs[:count]
    response, source, puts, picks = refs[count : count + 4]
    linked, slots, parts, crossed, outgoing, sems = refs[count + 4 :]
    unknowns, face = response.shape[1], slots.shape[2]
    small = [
        pltpu.make_async_copy(linked_hbm, linked, sems.at[0]),
        pltpu.make_async_copy(slots_hbm, slots, sems.at[1]),
        pltpu.make_async_copy(source_hbm, parts, sems.at[2]),
    ]
    large = [
        pltpu.make_async_copy(response_hbm.at[:, part, :], response.at[:, part, :], sems.at[3 + pos])
        for pos, part in enumerate(blocks(unknowns))
    ]
    for copy in small + large:
        copy.start()
    for copy in small:
        copy.wait()
    where = [lax.axis_index(axis) for axis in AXES]
    ids = [face_id(where, pos, phase) for pos, phase in rounds]
    rows = [slots[face_pos] for face_pos in ids]
    source[...] = join(parts[0], parts[1])
    crossed[...] = turned(source)
    upright = jnp.transpose(jnp.concatenate(rows + [rows[0]] * (-count % 8), axis=0))
    gates = [
        jnp.logical_and(linked[face_pos] != 0, has_neighbour(sizes, where, pos, phase))
        for face_pos, (pos, phase) in zip(ids, rounds)
    ]
    accepted = jnp.concatenate([jnp.where(gate, row, -1) for gate, row in zip(gates, rows)], axis=1)
    across = lax.broadcasted_iota(jnp.int32, (face, unknowns), 1)
    for pos in range(count):
        chosen = jnp.where(across == upright[:, pos : pos + 1], 1.0, 0.0)
        picks[pl.ds(pos * face, face), :] = chosen.astype(BF16)
    for part in blocks(unknowns):
        down = part.start + lax.broadcasted_iota(jnp.int32, (part.size, count * face), 0)
        puts[part, :] = jnp.where(down == accepted, 1.0, 0.0).astype(BF16)
    ready = 0
    for stage in STAGES:
        for copy in large[ready:stage]:
            copy.wait()
        for part in blocks(unknowns)[ready:stage]:
            respond(response, source, crossed, outgoing, part)
        ready = stage
    pick_faces(picks, outgoing, outs)


def sweep_kernel(count, response, source, puts, picks, *refs):
    arrived, outs = refs[:count], refs[count : 2 * count]
    values, straight, crossed, outgoing = refs[2 * count :]
    gather_values(arrived, values)
    for part in blocks(source.shape[0]):
        both = add_traces(puts, arrived, source, values, part)
        straight[part, :] = both
        crossed[part, :] = turned(both)
    for part in blocks(source.shape[0]):
        respond(response, straight, crossed, outgoing, part)
    pick_faces(picks, outgoing, outs)


def radiate_kernel(count, halves, eb, source, puts, radiation, *refs):
    arrived, outs = refs[:count], refs[count : count + 1 + halves]
    values, straight, crossed = refs[count + 1 + halves :]
    columns = source.shape[1] // 2
    gather_values(arrived, values)
    for part in blocks(source.shape[0]):
        both = add_traces(puts, arrived, source, values, part)
        straight[part, :] = both
        crossed[part, :] = turned(both)
    field = jnp.dot(radiation[0], straight[...], preferred_element_type=F32) + jnp.dot(
        radiation[1], crossed[...], preferred_element_type=F32
    )
    mine = lax.axis_index("gy") & 1
    for part in range(2):
        flat = jnp.transpose(field[:, part * columns : (part + 1) * columns])
        if not halves:
            outs[0][part] = flat
            continue
        split = [
            jnp.concatenate([flat[low : low + eb] for low in range(half * eb, columns, 2 * eb)], axis=0)
            for half in range(2)
        ]
        outs[0][part] = jnp.where(mine == 0, split[0], split[1])
        outs[1][part] = jnp.where(mine == 0, split[1], split[0])


def hbm_spec():
    return pl.BlockSpec(memory_space=pl.ANY)


def vmem_spec():
    return pl.BlockSpec(memory_space=pltpu.VMEM)


def in_hbm(value):
    return pltpu.with_memory_space_constraint(value, pltpu.HBM)


def in_vmem(value):
    return pltpu.with_memory_space_constraint(value, pltpu.VMEM)


def params():
    return pltpu.CompilerParams(vmem_limit_bytes=VMEM_LIMIT)


def first_sweep(sizes, rounds, linked, slots, source, response):
    unknowns, columns = source.shape[1:]
    face, count = slots.shape[2], len(rounds)
    kept = [
        (response.shape, BF16),
        ((unknowns, 2 * columns), BF16),
        ((unknowns, count * face), BF16),
        ((count * face, unknowns), BF16),
    ]
    outs = pl.pallas_call(
        functools.partial(first_kernel, sizes, rounds),
        out_shape=[jax.ShapeDtypeStruct((face, 2 * columns), BF16)] * count
        + [OUT_VMEM(shape, kind) for shape, kind in kept],
        in_specs=[hbm_spec()] * 4,
        out_specs=[vmem_spec()] * (count + len(kept)),
        scratch_shapes=[
            pltpu.SMEM(linked.shape, linked.dtype),
            pltpu.VMEM(slots.shape, slots.dtype),
            pltpu.VMEM(source.shape, BF16),
            pltpu.VMEM((unknowns, 2 * columns), BF16),
            pltpu.VMEM((unknowns, 2 * columns), BF16),
            pltpu.SemaphoreType.DMA((3 + CHUNKS,)),
        ],
        compiler_params=params(),
    )(in_hbm(linked), in_hbm(slots), in_hbm(source), in_hbm(response))
    return outs[:count], outs[count:]


def later_sweep(kept, arrived):
    response, source, puts, picks = kept
    count = len(arrived)
    return pl.pallas_call(
        functools.partial(sweep_kernel, count),
        out_shape=[jax.ShapeDtypeStruct(arrived[0].shape, BF16)] * count,
        in_specs=[vmem_spec()] * (4 + count),
        out_specs=[vmem_spec()] * count,
        scratch_shapes=[pltpu.VMEM((picks.shape[0], source.shape[1]), BF16)]
        + [pltpu.VMEM(source.shape, BF16)] * 3,
        compiler_params=params(),
    )(response, source, puts, picks, *arrived)


def radiate(kept, radiation, arrived, halves, eb):
    source, puts, picks = kept[1:]
    columns = source.shape[1] // 2
    angles = radiation.shape[1]
    count = len(arrived)
    shape = (2, columns // 2 if halves else columns, angles)
    outs = [jax.ShapeDtypeStruct(shape, F32)] * (1 + int(halves))
    return pl.pallas_call(
        functools.partial(radiate_kernel, count, int(halves), eb),
        out_shape=outs,
        in_specs=[vmem_spec()] * (3 + count),
        out_specs=[vmem_spec()] * len(outs),
        scratch_shapes=[pltpu.VMEM((picks.shape[0], source.shape[1]), BF16)]
        + [pltpu.VMEM(source.shape, BF16)] * 2,
        compiler_params=params(),
    )(source, puts, radiation, *arrived)


def bit_count(size):
    return size.bit_length() - 1


def mask_pairs(sizes, flips):
    pairs = []
    for at_x in range(sizes[0]):
        for at_y in range(sizes[1]):
            for at_z in range(sizes[2]):
                here = (at_x * sizes[1] + at_y) * sizes[2] + at_z
                there = ((at_x ^ flips[0]) * sizes[1] + (at_y ^ flips[1])) * sizes[2] + (at_z ^ flips[2])
                pairs.append((here, there))
    return pairs


def scatter_sum(parts, sizes, where, full):
    columns, angles = full
    bits = [bit_count(size) for size in sizes]
    halves = len(parts) > 1
    dims = {}
    shape = [2]
    for pos in (0, 1):
        for bit in reversed(range(bits[pos])):
            if halves and (pos, bit) == (1, 0):
                continue
            dims[(pos, bit)] = len(shape)
            shape.append(2)
    shape.append(columns // (sizes[0] * sizes[1]))
    for bit in reversed(range(bits[2])):
        dims[(2, bit)] = len(shape)
        shape.append(2)
    shape.append(angles // sizes[2])
    total = parts[0]
    if halves:
        total = total + lax.ppermute(parts[1], AXES, mask_pairs(sizes, (0, 1, 0)))
    total = total.reshape(shape)
    rest = [item for item in dims if item[0] != 0]
    rest = sorted(rest, key=lambda item: (item[1], item[0])) + sorted(item for item in dims if item[0] == 0)
    rounds = [rest[pos : pos + 2] for pos in range(0, len(rest), 2)]
    for order, group in enumerate(rounds):
        wide = order == len(rounds) - 1

        def taken(code):
            piece = total
            for place, (pos, bit) in enumerate(group):
                mine = (where[pos] >> bit) & 1
                piece = lax.dynamic_slice_in_dim(piece, mine ^ ((code >> place) & 1), 1, axis=dims[(pos, bit)])
            return piece

        got = []
        for code in reversed(range(1, 2 ** len(group))):
            flips = [0, 0, 0]
            for place, (pos, bit) in enumerate(group):
                flips[pos] |= ((code >> place) & 1) << bit
            piece = taken(code) if wide else taken(code).astype(BF16)
            got.append(lax.ppermute(piece, AXES, mask_pairs(sizes, flips)))
        total = taken(0)
        for piece in got:
            total = total + piece.astype(F32)
    return total.reshape(2, columns // (sizes[0] * sizes[1]), angles // sizes[2])


def shards(sizes, incident, response, radiation, face_index, linked):
    source = incident[0, 0, 0]
    response_mat = response[0, 0, 0]
    radiation_mat = radiation[0, 0, 0]
    slots = face_index[0, 0, 0][:, None, :]
    where = [lax.axis_index(axis) for axis in AXES]
    rounds = swap_rounds(sizes)
    columns, angles = source.shape[2], radiation_mat.shape[1]
    faces, kept = first_sweep(sizes, rounds, linked[0, 0, 0], slots, source, response_mat)
    for turn in range(ITERS):
        arrived = [
            lax.ppermute(face, AXES, swap_pairs(sizes, pos, phase))
            for face, (pos, phase) in zip(faces, rounds)
        ]
        if turn < ITERS - 1:
            faces = later_sweep(kept, arrived)
    halves = sizes[1] % 2 == 0
    parts = radiate(kept, radiation_mat, arrived, halves, columns // (sizes[0] * sizes[1]))
    return scatter_sum(parts, sizes, where, (columns, angles))


def solution(mesh):
    sizes = tuple(mesh.shape[axis] for axis in AXES)
    return jax.shard_map(
        functools.partial(shards, sizes),
        mesh=mesh,
        in_specs=(
            P("gx", "gy", "gz", None, None, None),
            P("gx", "gy", "gz", None, None, None),
            P("gx", "gy", "gz", None, None, None),
            P("gx", "gy", "gz", None, None),
            P("gx", "gy", "gz", None),
        ),
        out_specs=P(None, ("gx", "gy"), "gz"),
        check_vma=False,
    )
```

```python
import functools

import jax
import jax.numpy as jnp
from jax import lax
from jax.experimental import pallas as pl
from jax.experimental.pallas import tpu as pltpu
from jax.sharding import PartitionSpec as P

ITERS = 2
AXES = ("gx", "gy", "gz")
F32 = jnp.float32
BF16 = jnp.bfloat16
CHUNKS = 8
STAGES = (4, 6, 8)
VMEM_LIMIT = 40 * 1024 * 1024
OUT_VMEM = pltpu.VMEM


def swap_rounds(sizes):
    rounds = [(pos, phase) for pos in (0, 2) for phase in (0, 1)] + [(1, 1), (1, 0)]
    return [(pos, phase) for pos, phase in rounds if sizes[pos] > 1 + phase]


def partner_of(sizes, pos, phase, here):
    there = list(here)
    near = here[pos] + (1 if (here[pos] + phase) % 2 == 0 else -1)
    if 0 <= near < sizes[pos]:
        there[pos] = near
    elif pos == 1 or sizes[1] % 2:
        there[pos] = sizes[pos] - 1 - here[pos]
    else:
        there[1] = here[1] ^ 1
    return there


def swap_pairs(sizes, pos, phase):
    pairs = []
    for at_x in range(sizes[0]):
        for at_y in range(sizes[1]):
            for at_z in range(sizes[2]):
                there = partner_of(sizes, pos, phase, (at_x, at_y, at_z))
                if there != [at_x, at_y, at_z]:
                    pairs.append(
                        ((at_x * sizes[1] + at_y) * sizes[2] + at_z, (there[0] * sizes[1] + there[1]) * sizes[2] + there[2])
                    )
    return pairs


def has_neighbour(sizes, where, pos, phase):
    near = where[pos] + 1 - 2 * ((where[pos] + phase) & 1)
    return jnp.logical_and(near >= 0, near < sizes[pos])


def face_id(where, pos, phase):
    return 2 * pos + 1 - ((where[pos] + phase) & 1)


def join(left, right):
    return jnp.concatenate([left, right], axis=1)


def blocks(total):
    return [pl.ds(pos * (total // CHUNKS), total // CHUNKS) for pos in range(CHUNKS)]


def respond(response, straight, crossed, outgoing, part):
    outgoing[part, :] = (
        jnp.dot(response[0, part, :], straight[...], preferred_element_type=F32)
        + jnp.dot(response[1, part, :], crossed[...], preferred_element_type=F32)
    ).astype(BF16)


def pick_faces(picks, outgoing, outs):
    face = outs[0].shape[0]
    chosen = jnp.dot(picks[...], outgoing[...], preferred_element_type=F32).astype(BF16)
    for pos, out in enumerate(outs):
        out[...] = chosen[pos * face : (pos + 1) * face]


def add_traces(puts, arrived, source, values, part):
    traces = jnp.dot(puts[part, :], values[...], preferred_element_type=F32)
    return (traces + source[part, :].astype(F32)).astype(BF16)


def gather_values(arrived, values):
    face = arrived[0].shape[0]
    for pos, faces in enumerate(arrived):
        values[pl.ds(pos * face, face), :] = faces[...]


def turned(both):
    columns = both.shape[1] // 2
    return join(-both[:, columns:], both[:, :columns])


def first_kernel(sizes, rounds, linked_hbm, slots_hbm, source_hbm, response_hbm, *refs):
    count = len(rounds)
    outs = refs[:count]
    response, source, puts, picks = refs[count : count + 4]
    linked, slots, parts, crossed, outgoing, sems = refs[count + 4 :]
    unknowns, face = response.shape[1], slots.shape[2]
    small = [
        pltpu.make_async_copy(linked_hbm, linked, sems.at[0]),
        pltpu.make_async_copy(slots_hbm, slots, sems.at[1]),
        pltpu.make_async_copy(source_hbm, parts, sems.at[2]),
    ]
    large = [
        pltpu.make_async_copy(response_hbm.at[:, part, :], response.at[:, part, :], sems.at[3 + pos])
        for pos, part in enumerate(blocks(unknowns))
    ]
    for copy in small + large:
        copy.start()
    for copy in small:
        copy.wait()
    where = [lax.axis_index(axis) for axis in AXES]
    ids = [face_id(where, pos, phase) for pos, phase in rounds]
    rows = [slots[face_pos] for face_pos in ids]
    source[...] = join(parts[0], parts[1])
    crossed[...] = turned(source)
    upright = jnp.transpose(jnp.concatenate(rows + [rows[0]] * (-count % 8), axis=0))
    gates = [
        jnp.logical_and(linked[face_pos] != 0, has_neighbour(sizes, where, pos, phase))
        for face_pos, (pos, phase) in zip(ids, rounds)
    ]
    accepted = jnp.concatenate([jnp.where(gate, row, -1) for gate, row in zip(gates, rows)], axis=1)
    across = lax.broadcasted_iota(jnp.int32, (face, unknowns), 1)
    for pos in range(count):
        chosen = jnp.where(across == upright[:, pos : pos + 1], 1.0, 0.0)
        picks[pl.ds(pos * face, face), :] = chosen.astype(BF16)
    for part in blocks(unknowns):
        down = part.start + lax.broadcasted_iota(jnp.int32, (part.size, count * face), 0)
        puts[part, :] = jnp.where(down == accepted, 1.0, 0.0).astype(BF16)
    ready = 0
    for stage in STAGES:
        for copy in large[ready:stage]:
            copy.wait()
        for part in blocks(unknowns)[ready:stage]:
            respond(response, source, crossed, outgoing, part)
        ready = stage
    pick_faces(picks, outgoing, outs)


def sweep_kernel(count, response, source, puts, picks, *refs):
    arrived, outs = refs[:count], refs[count : 2 * count]
    values, straight, crossed, outgoing = refs[2 * count :]
    gather_values(arrived, values)
    for part in blocks(source.shape[0]):
        both = add_traces(puts, arrived, source, values, part)
        straight[part, :] = both
        crossed[part, :] = turned(both)
    for part in blocks(source.shape[0]):
        respond(response, straight, crossed, outgoing, part)
    pick_faces(picks, outgoing, outs)


def tint(at_x, at_y):
    return (at_x ^ (at_y >> 1)) & 1


def half_starts(sizes, half, eb, columns):
    chips = sizes[1] // 2
    return [(2 * pos + (half ^ tint(pos // chips, 2 * (pos % chips)))) * eb for pos in range(columns // (2 * eb))]


def radiate_kernel(sizes, count, halves, eb, source, puts, radiation, *refs):
    arrived, outs = refs[:count], refs[count : count + 1 + halves]
    values, straight, crossed = refs[count + 1 + halves :]
    columns = source.shape[1] // 2
    gather_values(arrived, values)
    for part in blocks(source.shape[0]):
        both = add_traces(puts, arrived, source, values, part)
        straight[part, :] = both
        crossed[part, :] = turned(both)
    field = jnp.dot(radiation[0], straight[...], preferred_element_type=F32) + jnp.dot(
        radiation[1], crossed[...], preferred_element_type=F32
    )
    along, across = lax.axis_index("gy"), lax.axis_index("gx")
    mine = (along & 1) ^ tint(across, along)
    for part in range(2):
        flat = jnp.transpose(field[:, part * columns : (part + 1) * columns])
        if not halves:
            outs[0][part] = flat
            continue
        split = [
            jnp.concatenate([flat[start : start + eb] for start in half_starts(sizes, half, eb, columns)], axis=0)
            for half in range(2)
        ]
        outs[0][part] = jnp.where(mine == 0, split[0], split[1])
        outs[1][part] = jnp.where(mine == 0, split[1], split[0])


def hbm_spec():
    return pl.BlockSpec(memory_space=pl.ANY)


def vmem_spec():
    return pl.BlockSpec(memory_space=pltpu.VMEM)


def in_hbm(value):
    return pltpu.with_memory_space_constraint(value, pltpu.HBM)


def in_vmem(value):
    return pltpu.with_memory_space_constraint(value, pltpu.VMEM)


def params():
    return pltpu.CompilerParams(vmem_limit_bytes=VMEM_LIMIT)


def first_sweep(sizes, rounds, linked, slots, source, response):
    unknowns, columns = source.shape[1:]
    face, count = slots.shape[2], len(rounds)
    kept = [
        (response.shape, BF16),
        ((unknowns, 2 * columns), BF16),
        ((unknowns, count * face), BF16),
        ((count * face, unknowns), BF16),
    ]
    outs = pl.pallas_call(
        functools.partial(first_kernel, sizes, rounds),
        out_shape=[jax.ShapeDtypeStruct((face, 2 * columns), BF16)] * count
        + [OUT_VMEM(shape, kind) for shape, kind in kept],
        in_specs=[hbm_spec()] * 4,
        out_specs=[vmem_spec()] * (count + len(kept)),
        scratch_shapes=[
            pltpu.SMEM(linked.shape, linked.dtype),
            pltpu.VMEM(slots.shape, slots.dtype),
            pltpu.VMEM(source.shape, BF16),
            pltpu.VMEM((unknowns, 2 * columns), BF16),
            pltpu.VMEM((unknowns, 2 * columns), BF16),
            pltpu.SemaphoreType.DMA((3 + CHUNKS,)),
        ],
        compiler_params=params(),
    )(in_hbm(linked), in_hbm(slots), in_hbm(source), in_hbm(response))
    return outs[:count], outs[count:]


def later_sweep(kept, arrived):
    response, source, puts, picks = kept
    count = len(arrived)
    return pl.pallas_call(
        functools.partial(sweep_kernel, count),
        out_shape=[jax.ShapeDtypeStruct(arrived[0].shape, BF16)] * count,
        in_specs=[vmem_spec()] * (4 + count),
        out_specs=[vmem_spec()] * count,
        scratch_shapes=[pltpu.VMEM((picks.shape[0], source.shape[1]), BF16)]
        + [pltpu.VMEM(source.shape, BF16)] * 3,
        compiler_params=params(),
    )(response, source, puts, picks, *arrived)


def radiate(sizes, kept, radiation, arrived, halves, eb):
    source, puts, picks = kept[1:]
    columns = source.shape[1] // 2
    angles = radiation.shape[1]
    count = len(arrived)
    shape = (2, columns // 2 if halves else columns, angles)
    outs = [jax.ShapeDtypeStruct(shape, F32)] * (1 + int(halves))
    return pl.pallas_call(
        functools.partial(radiate_kernel, sizes, count, int(halves), eb),
        out_shape=outs,
        in_specs=[vmem_spec()] * (3 + count),
        out_specs=[vmem_spec()] * len(outs),
        scratch_shapes=[pltpu.VMEM((picks.shape[0], source.shape[1]), BF16)]
        + [pltpu.VMEM(source.shape, BF16)] * 2,
        compiler_params=params(),
    )(source, puts, radiation, *arrived)


def bit_count(size):
    return size.bit_length() - 1


def mask_pairs(sizes, flips):
    pairs = []
    for at_x in range(sizes[0]):
        for at_y in range(sizes[1]):
            for at_z in range(sizes[2]):
                here = (at_x * sizes[1] + at_y) * sizes[2] + at_z
                there = ((at_x ^ flips[0]) * sizes[1] + (at_y ^ flips[1])) * sizes[2] + (at_z ^ flips[2])
                pairs.append((here, there))
    return pairs


def scatter_sum(parts, sizes, where, full):
    columns, angles = full
    bits = [bit_count(size) for size in sizes]
    halves = len(parts) > 1
    dims = {}
    shape = [2]
    for pos in (0, 1):
        for bit in reversed(range(bits[pos])):
            if halves and (pos, bit) == (1, 0):
                continue
            dims[(pos, bit)] = len(shape)
            shape.append(2)
    shape.append(columns // (sizes[0] * sizes[1]))
    for bit in reversed(range(bits[2])):
        dims[(2, bit)] = len(shape)
        shape.append(2)
    shape.append(angles // sizes[2])
    total = parts[0]
    if halves:
        total = total + lax.ppermute(parts[1], AXES, mask_pairs(sizes, (0, 1, 0)))
    total = total.reshape(shape)
    rest = [item for item in dims if item[0] != 0]
    rest = sorted(rest, key=lambda item: (item[1], item[0])) + sorted(item for item in dims if item[0] == 0)
    rounds = [rest[pos : pos + 2] for pos in range(0, len(rest), 2)]
    for order, group in enumerate(rounds):
        wide = order == len(rounds) - 1

        def taken(code):
            piece = total
            for place, (pos, bit) in enumerate(group):
                mine = (where[pos] >> bit) & 1
                piece = lax.dynamic_slice_in_dim(piece, mine ^ ((code >> place) & 1), 1, axis=dims[(pos, bit)])
            return piece

        got = []
        for code in reversed(range(1, 2 ** len(group))):
            flips = [0, 0, 0]
            for place, (pos, bit) in enumerate(group):
                flips[pos] |= ((code >> place) & 1) << bit
            if halves:
                flips[1] ^= tint(flips[0], flips[1])
            piece = taken(code) if wide else taken(code).astype(BF16)
            got.append(lax.ppermute(piece, AXES, mask_pairs(sizes, flips)))
        total = taken(0)
        for piece in got:
            total = total + piece.astype(F32)
    return total.reshape(2, columns // (sizes[0] * sizes[1]), angles // sizes[2])


def shards(sizes, incident, response, radiation, face_index, linked):
    source = incident[0, 0, 0]
    response_mat = response[0, 0, 0]
    radiation_mat = radiation[0, 0, 0]
    slots = face_index[0, 0, 0][:, None, :]
    where = [lax.axis_index(axis) for axis in AXES]
    rounds = swap_rounds(sizes)
    columns, angles = source.shape[2], radiation_mat.shape[1]
    faces, kept = first_sweep(sizes, rounds, linked[0, 0, 0], slots, source, response_mat)
    for turn in range(ITERS):
        arrived = [
            lax.ppermute(face, AXES, swap_pairs(sizes, pos, phase))
            for face, (pos, phase) in zip(faces, rounds)
        ]
        if turn < ITERS - 1:
            faces = later_sweep(kept, arrived)
    halves = sizes[1] % 2 == 0
    parts = radiate(sizes, kept, radiation_mat, arrived, halves, columns // (sizes[0] * sizes[1]))
    return scatter_sum(parts, sizes, where, (columns, angles))


def solution(mesh):
    sizes = tuple(mesh.shape[axis] for axis in AXES)
    return jax.shard_map(
        functools.partial(shards, sizes),
        mesh=mesh,
        in_specs=(
            P("gx", "gy", "gz", None, None, None),
            P("gx", "gy", "gz", None, None, None),
            P("gx", "gy", "gz", None, None, None),
            P("gx", "gy", "gz", None, None),
            P("gx", "gy", "gz", None),
        ),
        out_specs=P(None, ("gx", "gy"), "gz"),
        check_vma=False,
    )
```

```python
import functools

import jax
import jax.numpy as jnp
from jax import lax
from jax.experimental import pallas as pl
from jax.experimental.pallas import tpu as pltpu
from jax.sharding import PartitionSpec as P

ITERS = 2
AXES = ("gx", "gy", "gz")
F32 = jnp.float32
BF16 = jnp.bfloat16
CHUNKS = 8
STAGES = (4, 6, 8)
VMEM_LIMIT = 40 * 1024 * 1024
OUT_VMEM = pltpu.VMEM


def swap_rounds(sizes):
    rounds = [(2,0),(2,1),(0,0),(0,1),(1,1),(1,0)]
    return [(pos, phase) for pos, phase in rounds if sizes[pos] > 1 + phase]


def partner_of(sizes, pos, phase, here):
    there = list(here)
    near = here[pos] + (1 if (here[pos] + phase) % 2 == 0 else -1)
    if 0 <= near < sizes[pos]:
        there[pos] = near
    elif pos == 1:
        there[0] = here[0] ^ 1
    elif sizes[1] % 2:
        there[pos] = sizes[pos] - 1 - here[pos]
    else:
        there[1] = here[1] ^ 1
    return there


def swap_pairs(sizes, pos, phase):
    pairs = []
    for at_x in range(sizes[0]):
        for at_y in range(sizes[1]):
            for at_z in range(sizes[2]):
                there = partner_of(sizes, pos, phase, (at_x, at_y, at_z))
                if there != [at_x, at_y, at_z]:
                    pairs.append(
                        ((at_x * sizes[1] + at_y) * sizes[2] + at_z, (there[0] * sizes[1] + there[1]) * sizes[2] + there[2])
                    )
    return pairs


def has_neighbour(sizes, where, pos, phase):
    near = where[pos] + 1 - 2 * ((where[pos] + phase) & 1)
    return jnp.logical_and(near >= 0, near < sizes[pos])


def face_id(where, pos, phase):
    return 2 * pos + 1 - ((where[pos] + phase) & 1)


def join(left, right):
    return jnp.concatenate([left, right], axis=1)


def blocks(total):
    return [pl.ds(pos * (total // CHUNKS), total // CHUNKS) for pos in range(CHUNKS)]


def respond(response, straight, crossed, outgoing, part):
    outgoing[part, :] = (
        jnp.dot(response[0, part, :], straight[...], preferred_element_type=F32)
        + jnp.dot(response[1, part, :], crossed[...], preferred_element_type=F32)
    ).astype(BF16)


def pick_faces(picks, outgoing, outs):
    face = outs[0].shape[0]
    chosen = jnp.dot(picks[...], outgoing[...], preferred_element_type=F32).astype(BF16)
    for pos, out in enumerate(outs):
        out[...] = chosen[pos * face : (pos + 1) * face]


def add_traces(puts, arrived, source, values, part):
    traces = jnp.dot(puts[part, :], values[...], preferred_element_type=F32)
    return (traces + source[part, :].astype(F32)).astype(BF16)


def gather_values(arrived, values):
    face = arrived[0].shape[0]
    for pos, faces in enumerate(arrived):
        values[pl.ds(pos * face, face), :] = faces[...]


def turned(both):
    columns = both.shape[1] // 2
    return join(-both[:, columns:], both[:, :columns])


def first_kernel(sizes, rounds, linked_hbm, slots_hbm, source_hbm, response_hbm, *refs):
    count = len(rounds)
    outs = refs[:count]
    response, source, puts, picks = refs[count : count + 4]
    linked, slots, parts, crossed, outgoing, sems = refs[count + 4 :]
    unknowns, face = response.shape[1], slots.shape[2]
    small = [
        pltpu.make_async_copy(linked_hbm, linked, sems.at[0]),
        pltpu.make_async_copy(slots_hbm, slots, sems.at[1]),
        pltpu.make_async_copy(source_hbm, parts, sems.at[2]),
    ]
    large = [
        pltpu.make_async_copy(response_hbm.at[:, part, :], response.at[:, part, :], sems.at[3 + pos])
        for pos, part in enumerate(blocks(unknowns))
    ]
    for copy in small + large:
        copy.start()
    for copy in small:
        copy.wait()
    where = [lax.axis_index(axis) for axis in AXES]
    ids = [face_id(where, pos, phase) for pos, phase in rounds]
    rows = [slots[face_pos] for face_pos in ids]
    source[...] = join(parts[0], parts[1])
    crossed[...] = turned(source)
    upright = jnp.transpose(jnp.concatenate(rows + [rows[0]] * (-count % 8), axis=0))
    gates = [
        jnp.logical_and(linked[face_pos] != 0, has_neighbour(sizes, where, pos, phase))
        for face_pos, (pos, phase) in zip(ids, rounds)
    ]
    accepted = jnp.concatenate([jnp.where(gate, row, -1) for gate, row in zip(gates, rows)], axis=1)
    across = lax.broadcasted_iota(jnp.int32, (face, unknowns), 1)
    for pos in range(count):
        chosen = jnp.where(across == upright[:, pos : pos + 1], 1.0, 0.0)
        picks[pl.ds(pos * face, face), :] = chosen.astype(BF16)
    for part in blocks(unknowns):
        down = part.start + lax.broadcasted_iota(jnp.int32, (part.size, count * face), 0)
        puts[part, :] = jnp.where(down == accepted, 1.0, 0.0).astype(BF16)
    ready = 0
    for stage in STAGES:
        for copy in large[ready:stage]:
            copy.wait()
        for part in blocks(unknowns)[ready:stage]:
            respond(response, source, crossed, outgoing, part)
        ready = stage
    pick_faces(picks, outgoing, outs)


def sweep_kernel(count, response, source, puts, picks, *refs):
    arrived, outs = refs[:count], refs[count : 2 * count]
    values, straight, crossed, outgoing = refs[2 * count :]
    gather_values(arrived, values)
    for part in blocks(source.shape[0]):
        both = add_traces(puts, arrived, source, values, part)
        straight[part, :] = both
        crossed[part, :] = turned(both)
    for part in blocks(source.shape[0]):
        respond(response, straight, crossed, outgoing, part)
    pick_faces(picks, outgoing, outs)


def tint(at_x, at_y):
    return (at_x ^ (at_y >> 1)) & 1


def half_starts(sizes, half, eb, columns):
    chips = sizes[1] // 2
    return [(2 * pos + (half ^ tint(pos // chips, 2 * (pos % chips)))) * eb for pos in range(columns // (2 * eb))]


def columns_kernel(part, radiation, puts, out):
    out[...] = jnp.dot(radiation[part], puts[...], preferred_element_type=F32).astype(BF16)


def incident_kernel(radiation, source, puts, base, out):
    columns_kernel(1, radiation, puts, out)
    base[...] = jnp.dot(radiation[0], source[...], preferred_element_type=F32) + jnp.dot(
        radiation[1], turned(source[...]), preferred_element_type=F32
    )


def radiate_kernel(sizes, count, halves, eb, base, placed, placed_imag, *refs):
    arrived, outs = refs[:count], refs[count : count + 1 + halves]
    (values,) = refs[count + 1 + halves :]
    columns = base.shape[1] // 2
    gather_values(arrived, values)
    field = (
        base[...]
        + jnp.dot(placed[...], values[...], preferred_element_type=F32)
        + jnp.dot(placed_imag[...], turned(values[...]), preferred_element_type=F32)
    )
    along, across = lax.axis_index("gy"), lax.axis_index("gx")
    mine = (along & 1) ^ tint(across, along)
    for part in range(2):
        flat = jnp.transpose(field[:, part * columns : (part + 1) * columns])
        if not halves:
            outs[0][part] = flat
            continue
        split = [
            jnp.concatenate([flat[start : start + eb] for start in half_starts(sizes, half, eb, columns)], axis=0)
            for half in range(2)
        ]
        outs[0][part] = jnp.where(mine == 0, split[0], split[1])
        outs[1][part] = jnp.where(mine == 0, split[1], split[0])


def hbm_spec():
    return pl.BlockSpec(memory_space=pl.ANY)


def vmem_spec():
    return pl.BlockSpec(memory_space=pltpu.VMEM)


def in_hbm(value):
    return pltpu.with_memory_space_constraint(value, pltpu.HBM)


def in_vmem(value):
    return pltpu.with_memory_space_constraint(value, pltpu.VMEM)


def params():
    return pltpu.CompilerParams(vmem_limit_bytes=VMEM_LIMIT)


def first_sweep(sizes, rounds, linked, slots, source, response):
    unknowns, columns = source.shape[1:]
    face, count = slots.shape[2], len(rounds)
    kept = [
        (response.shape, BF16),
        ((unknowns, 2 * columns), BF16),
        ((unknowns, count * face), BF16),
        ((count * face, unknowns), BF16),
    ]
    outs = pl.pallas_call(
        functools.partial(first_kernel, sizes, rounds),
        out_shape=[jax.ShapeDtypeStruct((face, 2 * columns), BF16)] * count
        + [OUT_VMEM(shape, kind) for shape, kind in kept],
        in_specs=[hbm_spec()] * 4,
        out_specs=[vmem_spec()] * (count + len(kept)),
        scratch_shapes=[
            pltpu.SMEM(linked.shape, linked.dtype),
            pltpu.VMEM(slots.shape, slots.dtype),
            pltpu.VMEM(source.shape, BF16),
            pltpu.VMEM((unknowns, 2 * columns), BF16),
            pltpu.VMEM((unknowns, 2 * columns), BF16),
            pltpu.SemaphoreType.DMA((3 + CHUNKS,)),
        ],
        compiler_params=params(),
    )(in_hbm(linked), in_hbm(slots), in_hbm(source), in_hbm(response))
    return outs[:count], outs[count:]


def later_sweep(kept, arrived):
    response, source, puts, picks = kept
    count = len(arrived)
    return pl.pallas_call(
        functools.partial(sweep_kernel, count),
        out_shape=[jax.ShapeDtypeStruct(arrived[0].shape, BF16)] * count,
        in_specs=[vmem_spec()] * (4 + count),
        out_specs=[vmem_spec()] * count,
        scratch_shapes=[pltpu.VMEM((picks.shape[0], source.shape[1]), BF16)]
        + [pltpu.VMEM(source.shape, BF16)] * 3,
        compiler_params=params(),
    )(response, source, puts, picks, *arrived)


def cost(rows, depth, columns):
    moved = 2 * (rows * depth + depth * columns + rows * columns)
    return pl.CostEstimate(flops=2 * rows * depth * columns, bytes_accessed=moved, transcendentals=0)


def placed_real(radiation, puts):
    shape = (radiation.shape[1], puts.shape[1])
    return pl.pallas_call(
        functools.partial(columns_kernel, 0),
        out_shape=OUT_VMEM(shape, BF16),
        in_specs=[vmem_spec()] * 2,
        out_specs=vmem_spec(),
        cost_estimate=cost(shape[0], *puts.shape),
        compiler_params=params(),
    )(radiation, puts)


def placed_imag_and_incident(radiation, source, puts):
    angles = radiation.shape[1]
    return pl.pallas_call(
        incident_kernel,
        out_shape=[OUT_VMEM((angles, source.shape[1]), F32), OUT_VMEM((angles, puts.shape[1]), BF16)],
        in_specs=[vmem_spec()] * 3,
        out_specs=[vmem_spec()] * 2,
        cost_estimate=cost(2 * angles, *puts.shape),
        compiler_params=params(),
    )(radiation, source, puts)


def radiate(sizes, base, placed, placed_imag, arrived, halves, eb):
    columns = base.shape[1] // 2
    angles = base.shape[0]
    count = len(arrived)
    shape = (2, columns // 2 if halves else columns, angles)
    outs = [jax.ShapeDtypeStruct(shape, F32)] * (1 + int(halves))
    return pl.pallas_call(
        functools.partial(radiate_kernel, sizes, count, int(halves), eb),
        out_shape=outs,
        in_specs=[vmem_spec()] * (3 + count),
        out_specs=[vmem_spec()] * len(outs),
        scratch_shapes=[pltpu.VMEM((placed.shape[1], 2 * columns), BF16)],
        compiler_params=params(),
    )(base, placed, placed_imag, *arrived)


def bit_count(size):
    return size.bit_length() - 1


def mask_pairs(sizes, flips):
    pairs = []
    for at_x in range(sizes[0]):
        for at_y in range(sizes[1]):
            for at_z in range(sizes[2]):
                here = (at_x * sizes[1] + at_y) * sizes[2] + at_z
                there = ((at_x ^ flips[0]) * sizes[1] + (at_y ^ flips[1])) * sizes[2] + (at_z ^ flips[2])
                pairs.append((here, there))
    return pairs


def scatter_sum(parts, sizes, where, full):
    columns, angles = full
    bits = [bit_count(size) for size in sizes]
    halves = len(parts) > 1
    dims = {}
    shape = [2]
    for pos in (0, 1):
        for bit in reversed(range(bits[pos])):
            if halves and (pos, bit) == (1, 0):
                continue
            dims[(pos, bit)] = len(shape)
            shape.append(2)
    shape.append(columns // (sizes[0] * sizes[1]))
    for bit in reversed(range(bits[2])):
        dims[(2, bit)] = len(shape)
        shape.append(2)
    shape.append(angles // sizes[2])
    total = parts[0]
    if halves:
        total = total + lax.ppermute(parts[1], AXES, mask_pairs(sizes, (0, 1, 0)))
    total = total.reshape(shape)
    rest = [item for item in dims if item[0] != 0]
    rest = sorted(rest, key=lambda item: (item[1], item[0])) + sorted(item for item in dims if item[0] == 0)
    rounds = [rest[pos : pos + 2] for pos in range(0, len(rest), 2)]
    for order, group in enumerate(rounds):
        wide = order == len(rounds) - 1

        def taken(code):
            piece = total
            for place, (pos, bit) in enumerate(group):
                mine = (where[pos] >> bit) & 1
                piece = lax.dynamic_slice_in_dim(piece, mine ^ ((code >> place) & 1), 1, axis=dims[(pos, bit)])
            return piece

        got = []
        for code in reversed(range(1, 2 ** len(group))):
            flips = [0, 0, 0]
            for place, (pos, bit) in enumerate(group):
                flips[pos] |= ((code >> place) & 1) << bit
            if halves:
                flips[1] ^= tint(flips[0], flips[1])
            piece = taken(code) if wide else taken(code).astype(BF16)
            got.append(lax.ppermute(piece, AXES, mask_pairs(sizes, flips)))
        total = taken(0)
        for piece in got:
            total = total + piece.astype(F32)
    return total.reshape(2, columns // (sizes[0] * sizes[1]), angles // sizes[2])


def shards(sizes, incident, response, radiation, face_index, linked):
    source = incident[0, 0, 0]
    response_mat = response[0, 0, 0]
    radiation_mat = radiation[0, 0, 0]
    slots = face_index[0, 0, 0][:, None, :]
    where = [lax.axis_index(axis) for axis in AXES]
    rounds = swap_rounds(sizes)
    columns, angles = source.shape[2], radiation_mat.shape[1]
    faces, kept = first_sweep(sizes, rounds, linked[0, 0, 0], slots, source, response_mat)
    placed = placed_real(radiation_mat, kept[2])
    for turn in range(ITERS):
        if turn == ITERS - 1:
            source_now, puts_now, faces = lax.optimization_barrier((kept[1], kept[2], list(faces)))
            base, placed_imag = placed_imag_and_incident(radiation_mat, source_now, puts_now)
        arrived = [
            lax.ppermute(face, AXES, swap_pairs(sizes, pos, phase))
            for face, (pos, phase) in zip(faces, rounds)
        ]
        if turn == 0:
            placed, arrived = lax.optimization_barrier((placed, arrived))
        if turn < ITERS - 1:
            faces = later_sweep(kept, arrived)
    halves = sizes[1] % 2 == 0
    parts = radiate(sizes, base, placed, placed_imag, arrived, halves, columns // (sizes[0] * sizes[1]))
    return scatter_sum(parts, sizes, where, (columns, angles))


def solution(mesh):
    sizes = tuple(mesh.shape[axis] for axis in AXES)
    return jax.shard_map(
        functools.partial(shards, sizes),
        mesh=mesh,
        in_specs=(
            P("gx", "gy", "gz", None, None, None),
            P("gx", "gy", "gz", None, None, None),
            P("gx", "gy", "gz", None, None, None),
            P("gx", "gy", "gz", None, None),
            P("gx", "gy", "gz", None),
        ),
        out_specs=P(None, ("gx", "gy"), "gz"),
        check_vma=False,
    )
```

```python
import functools

import jax
import jax.numpy as jnp
from jax import lax
from jax.experimental import pallas as pl
from jax.experimental.pallas import tpu as pltpu
from jax.sharding import PartitionSpec as P

ITERS = 2
AXES = ("gx", "gy", "gz")
F32 = jnp.float32
BF16 = jnp.bfloat16
CHUNKS = 8
STAGES = (4, 6, 8)
VMEM_LIMIT = 40 * 1024 * 1024
OUT_VMEM = pltpu.VMEM


def swap_rounds(sizes):
    rounds = [(2, 0), (2, 1), (0, 0), (0, 1), (1, 1), (1, 0)]
    return [(pos, phase) for pos, phase in rounds if sizes[pos] > 1 + phase]


def partner_of(sizes, pos, phase, here):
    there = list(here)
    near = here[pos] + (1 if (here[pos] + phase) % 2 == 0 else -1)
    if 0 <= near < sizes[pos]:
        there[pos] = near
    elif pos == 1:
        there[0] = here[0] ^ 1
    elif sizes[1] % 2:
        there[pos] = sizes[pos] - 1 - here[pos]
    else:
        there[1] = here[1] ^ 1
    return there


def swap_pairs(sizes, pos, phase):
    pairs = []
    for at_x in range(sizes[0]):
        for at_y in range(sizes[1]):
            for at_z in range(sizes[2]):
                there = partner_of(sizes, pos, phase, (at_x, at_y, at_z))
                if there != [at_x, at_y, at_z]:
                    pairs.append(
                        ((at_x * sizes[1] + at_y) * sizes[2] + at_z, (there[0] * sizes[1] + there[1]) * sizes[2] + there[2])
                    )
    return pairs


def has_neighbour(sizes, where, pos, phase):
    near = where[pos] + 1 - 2 * ((where[pos] + phase) & 1)
    return jnp.logical_and(near >= 0, near < sizes[pos])


def face_id(where, pos, phase):
    return 2 * pos + 1 - ((where[pos] + phase) & 1)


def join(left, right):
    return jnp.concatenate([left, right], axis=1)


def blocks(total):
    return [pl.ds(pos * (total // CHUNKS), total // CHUNKS) for pos in range(CHUNKS)]


def respond(response, straight, crossed, outgoing, part):
    outgoing[part, :] = (
        jnp.dot(response[0, part, :], straight[...], preferred_element_type=F32)
        + jnp.dot(response[1, part, :], crossed[...], preferred_element_type=F32)
    ).astype(BF16)


def pick_faces(picks, outgoing, outs):
    face = outs[0].shape[0]
    chosen = jnp.dot(picks[...], outgoing[...], preferred_element_type=F32).astype(BF16)
    for pos, out in enumerate(outs):
        out[...] = chosen[pos * face : (pos + 1) * face]


def add_traces(puts, arrived, source, values, part):
    traces = jnp.dot(puts[part, :], values[...], preferred_element_type=F32)
    return (traces + source[part, :].astype(F32)).astype(BF16)


def gather_values(arrived, values):
    face = arrived[0].shape[0]
    for pos, faces in enumerate(arrived):
        values[pl.ds(pos * face, face), :] = faces[...]


def turned(both):
    columns = both.shape[1] // 2
    return join(-both[:, columns:], both[:, :columns])


def first_kernel(sizes, rounds, linked_hbm, slots_hbm, source_hbm, response_hbm, *refs):
    count = len(rounds)
    outs = refs[:count]
    response, source, puts, picks = refs[count : count + 4]
    linked, slots, parts, crossed, outgoing, sems = refs[count + 4 :]
    unknowns, face = response.shape[1], slots.shape[2]
    small = [
        pltpu.make_async_copy(linked_hbm, linked, sems.at[0]),
        pltpu.make_async_copy(slots_hbm, slots, sems.at[1]),
        pltpu.make_async_copy(source_hbm, parts, sems.at[2]),
    ]
    large = [
        pltpu.make_async_copy(response_hbm.at[:, part, :], response.at[:, part, :], sems.at[3 + pos])
        for pos, part in enumerate(blocks(unknowns))
    ]
    for copy in small + large:
        copy.start()
    for copy in small:
        copy.wait()
    where = [lax.axis_index(axis) for axis in AXES]
    ids = [face_id(where, pos, phase) for pos, phase in rounds]
    rows = [slots[face_pos] for face_pos in ids]
    source[...] = join(parts[0], parts[1])
    crossed[...] = turned(source)
    upright = jnp.transpose(jnp.concatenate(rows + [rows[0]] * (-count % 8), axis=0))
    gates = [
        jnp.logical_and(linked[face_pos] != 0, has_neighbour(sizes, where, pos, phase))
        for face_pos, (pos, phase) in zip(ids, rounds)
    ]
    accepted = jnp.concatenate([jnp.where(gate, row, -1) for gate, row in zip(gates, rows)], axis=1)
    across = lax.broadcasted_iota(jnp.int32, (face, unknowns), 1)
    for pos in range(count):
        chosen = jnp.where(across == upright[:, pos : pos + 1], 1.0, 0.0)
        picks[pl.ds(pos * face, face), :] = chosen.astype(BF16)
    for part in blocks(unknowns):
        down = part.start + lax.broadcasted_iota(jnp.int32, (part.size, count * face), 0)
        puts[part, :] = jnp.where(down == accepted, 1.0, 0.0).astype(BF16)
    ready = 0
    for stage in STAGES:
        for copy in large[ready:stage]:
            copy.wait()
        for part in blocks(unknowns)[ready:stage]:
            respond(response, source, crossed, outgoing, part)
        ready = stage
    pick_faces(picks, outgoing, outs)


def sweep_kernel(count, response, source, puts, picks, *refs):
    arrived, outs = refs[:count], refs[count : 2 * count]
    values, straight, crossed, outgoing = refs[2 * count :]
    gather_values(arrived, values)
    for part in blocks(source.shape[0]):
        both = add_traces(puts, arrived, source, values, part)
        straight[part, :] = both
        crossed[part, :] = turned(both)
    for part in blocks(source.shape[0]):
        respond(response, straight, crossed, outgoing, part)
    pick_faces(picks, outgoing, outs)


def tint(at_x, at_y):
    return ((at_x >> 1) ^ (at_y >> 1)) & 1


def half_starts(sizes, half, eb, columns):
    chips = sizes[1] // 2
    return [(2 * pos + (half ^ tint(pos // chips, 2 * (pos % chips)))) * eb for pos in range(columns // (2 * eb))]


def columns_kernel(part, radiation, puts, out):
    out[...] = jnp.dot(radiation[part], puts[...], preferred_element_type=F32).astype(BF16)


def incident_kernel(radiation, source, puts, base, out):
    columns_kernel(1, radiation, puts, out)
    base[...] = jnp.dot(radiation[0], source[...], preferred_element_type=F32) + jnp.dot(
        radiation[1], turned(source[...]), preferred_element_type=F32
    )


def radiate_kernel(sizes, count, halves, eb, base, placed, placed_imag, *refs):
    arrived, outs = refs[:count], refs[count : count + 1 + halves]
    (values,) = refs[count + 1 + halves :]
    columns = base.shape[1] // 2
    gather_values(arrived, values)
    field = (
        base[...]
        + jnp.dot(placed[...], values[...], preferred_element_type=F32)
        + jnp.dot(placed_imag[...], turned(values[...]), preferred_element_type=F32)
    )
    along, across = lax.axis_index("gy"), lax.axis_index("gx")
    mine = (along & 1) ^ tint(across, along)
    for part in range(2):
        flat = jnp.transpose(field[:, part * columns : (part + 1) * columns])
        if not halves:
            outs[0][part] = flat
            continue
        split = [
            jnp.concatenate([flat[start : start + eb] for start in half_starts(sizes, half, eb, columns)], axis=0)
            for half in range(2)
        ]
        outs[0][part] = jnp.where(mine == 0, split[0], split[1])
        outs[1][part] = jnp.where(mine == 0, split[1], split[0])


def hbm_spec():
    return pl.BlockSpec(memory_space=pl.ANY)


def vmem_spec():
    return pl.BlockSpec(memory_space=pltpu.VMEM)


def in_hbm(value):
    return pltpu.with_memory_space_constraint(value, pltpu.HBM)


def in_vmem(value):
    return pltpu.with_memory_space_constraint(value, pltpu.VMEM)


def params():
    return pltpu.CompilerParams(vmem_limit_bytes=VMEM_LIMIT)


def first_sweep(sizes, rounds, linked, slots, source, response):
    unknowns, columns = source.shape[1:]
    face, count = slots.shape[2], len(rounds)
    kept = [
        (response.shape, BF16),
        ((unknowns, 2 * columns), BF16),
        ((unknowns, count * face), BF16),
        ((count * face, unknowns), BF16),
    ]
    outs = pl.pallas_call(
        functools.partial(first_kernel, sizes, rounds),
        out_shape=[jax.ShapeDtypeStruct((face, 2 * columns), BF16)] * count
        + [OUT_VMEM(shape, kind) for shape, kind in kept],
        in_specs=[hbm_spec()] * 4,
        out_specs=[vmem_spec()] * (count + len(kept)),
        scratch_shapes=[
            pltpu.SMEM(linked.shape, linked.dtype),
            pltpu.VMEM(slots.shape, slots.dtype),
            pltpu.VMEM(source.shape, BF16),
            pltpu.VMEM((unknowns, 2 * columns), BF16),
            pltpu.VMEM((unknowns, 2 * columns), BF16),
            pltpu.SemaphoreType.DMA((3 + CHUNKS,)),
        ],
        compiler_params=params(),
    )(in_hbm(linked), in_hbm(slots), in_hbm(source), in_hbm(response))
    return outs[:count], outs[count:]


def later_sweep(kept, arrived):
    response, source, puts, picks = kept
    count = len(arrived)
    return pl.pallas_call(
        functools.partial(sweep_kernel, count),
        out_shape=[jax.ShapeDtypeStruct(arrived[0].shape, BF16)] * count,
        in_specs=[vmem_spec()] * (4 + count),
        out_specs=[vmem_spec()] * count,
        scratch_shapes=[pltpu.VMEM((picks.shape[0], source.shape[1]), BF16)]
        + [pltpu.VMEM(source.shape, BF16)] * 3,
        compiler_params=params(),
    )(response, source, puts, picks, *arrived)


def cost(rows, depth, columns):
    moved = 2 * (rows * depth + depth * columns + rows * columns)
    return pl.CostEstimate(flops=2 * rows * depth * columns, bytes_accessed=moved, transcendentals=0)


def placed_real(radiation, puts):
    shape = (radiation.shape[1], puts.shape[1])
    return pl.pallas_call(
        functools.partial(columns_kernel, 0),
        out_shape=OUT_VMEM(shape, BF16),
        in_specs=[vmem_spec()] * 2,
        out_specs=vmem_spec(),
        cost_estimate=cost(shape[0], *puts.shape),
        compiler_params=params(),
    )(radiation, puts)


def placed_imag_and_incident(radiation, source, puts):
    angles = radiation.shape[1]
    return pl.pallas_call(
        incident_kernel,
        out_shape=[OUT_VMEM((angles, source.shape[1]), F32), OUT_VMEM((angles, puts.shape[1]), BF16)],
        in_specs=[vmem_spec()] * 3,
        out_specs=[vmem_spec()] * 2,
        cost_estimate=cost(2 * angles, *puts.shape),
        compiler_params=params(),
    )(radiation, source, puts)


def radiate(sizes, base, placed, placed_imag, arrived, halves, eb):
    columns = base.shape[1] // 2
    angles = base.shape[0]
    count = len(arrived)
    shape = (2, columns // 2 if halves else columns, angles)
    outs = [jax.ShapeDtypeStruct(shape, F32)] * (1 + int(halves))
    return pl.pallas_call(
        functools.partial(radiate_kernel, sizes, count, int(halves), eb),
        out_shape=outs,
        in_specs=[vmem_spec()] * (3 + count),
        out_specs=[vmem_spec()] * len(outs),
        scratch_shapes=[pltpu.VMEM((placed.shape[1], 2 * columns), BF16)],
        compiler_params=params(),
    )(base, placed, placed_imag, *arrived)


def bit_count(size):
    return size.bit_length() - 1


def mask_pairs(sizes, flips):
    pairs = []
    for at_x in range(sizes[0]):
        for at_y in range(sizes[1]):
            for at_z in range(sizes[2]):
                here = (at_x * sizes[1] + at_y) * sizes[2] + at_z
                there = ((at_x ^ flips[0]) * sizes[1] + (at_y ^ flips[1])) * sizes[2] + (at_z ^ flips[2])
                pairs.append((here, there))
    return pairs


def scatter_sum(parts, sizes, where, full):
    columns, angles = full
    bits = [bit_count(size) for size in sizes]
    halves = len(parts) > 1
    dims = {}
    shape = [2]
    for pos in (0, 1):
        for bit in reversed(range(bits[pos])):
            if halves and (pos, bit) == (1, 0):
                continue
            dims[(pos, bit)] = len(shape)
            shape.append(2)
    shape.append(columns // (sizes[0] * sizes[1]))
    for bit in reversed(range(bits[2])):
        dims[(2, bit)] = len(shape)
        shape.append(2)
    shape.append(angles // sizes[2])
    total = parts[0]
    if halves:
        total = total + lax.ppermute(parts[1], AXES, mask_pairs(sizes, (0, 1, 0)))
    total = total.reshape(shape)
    rest = sorted(item for item in dims if item[0] != 0) + sorted((item for item in dims if item[0] == 0), reverse=True)
    rounds = [rest[pos : pos + 2] for pos in range(0, len(rest), 2)]
    for order, group in enumerate(rounds):
        wide = order == len(rounds) - 1

        def taken(code):
            piece = total
            for place, (pos, bit) in enumerate(group):
                mine = (where[pos] >> bit) & 1
                piece = lax.dynamic_slice_in_dim(piece, mine ^ ((code >> place) & 1), 1, axis=dims[(pos, bit)])
            return piece

        got = []
        for code in reversed(range(1, 2 ** len(group))):
            flips = [0, 0, 0]
            for place, (pos, bit) in enumerate(group):
                flips[pos] |= ((code >> place) & 1) << bit
            if halves:
                flips[1] ^= tint(flips[0], flips[1])
            piece = taken(code) if wide else taken(code).astype(BF16)
            got.append(lax.ppermute(piece, AXES, mask_pairs(sizes, flips)))
        total = taken(0)
        for piece in got:
            total = total + piece.astype(F32)
    return total.reshape(2, columns // (sizes[0] * sizes[1]), angles // sizes[2])


def shards(sizes, incident, response, radiation, face_index, linked):
    source = incident[0, 0, 0]
    response_mat = response[0, 0, 0]
    radiation_mat = radiation[0, 0, 0]
    slots = face_index[0, 0, 0][:, None, :]
    where = [lax.axis_index(axis) for axis in AXES]
    rounds = swap_rounds(sizes)
    columns, angles = source.shape[2], radiation_mat.shape[1]
    faces, kept = first_sweep(sizes, rounds, linked[0, 0, 0], slots, source, response_mat)
    placed = placed_real(radiation_mat, kept[2])
    for turn in range(ITERS):
        if turn == ITERS - 1:
            source_now, puts_now, faces = lax.optimization_barrier((kept[1], kept[2], list(faces)))
            base, placed_imag = placed_imag_and_incident(radiation_mat, source_now, puts_now)
        arrived = [
            lax.ppermute(face, AXES, swap_pairs(sizes, pos, phase))
            for face, (pos, phase) in zip(faces, rounds)
        ]
        if turn == 0:
            placed, arrived = lax.optimization_barrier((placed, arrived))
        if turn < ITERS - 1:
            faces = later_sweep(kept, arrived)
    halves = sizes[1] % 2 == 0
    parts = radiate(sizes, base, placed, placed_imag, arrived, halves, columns // (sizes[0] * sizes[1]))
    return scatter_sum(parts, sizes, where, (columns, angles))


def solution(mesh):
    sizes = tuple(mesh.shape[axis] for axis in AXES)
    return jax.shard_map(
        functools.partial(shards, sizes),
        mesh=mesh,
        in_specs=(
            P("gx", "gy", "gz", None, None, None),
            P("gx", "gy", "gz", None, None, None),
            P("gx", "gy", "gz", None, None, None),
            P("gx", "gy", "gz", None, None),
            P("gx", "gy", "gz", None),
        ),
        out_specs=P(None, ("gx", "gy"), "gz"),
        check_vma=False,
    )
```

```python
import functools

import jax
import jax.numpy as jnp
from jax import lax
from jax.experimental import pallas as pl
from jax.experimental.pallas import tpu as pltpu
from jax.sharding import PartitionSpec as P

ITERS = 2
AXES = ("gx", "gy", "gz")
F32 = jnp.float32
BF16 = jnp.bfloat16
CHUNKS = 10
STAGES = (6, 10)
VMEM_LIMIT = 40 * 1024 * 1024
OUT_VMEM = pltpu.VMEM


def swap_rounds(sizes):
    rounds = [(2, 0), (2, 1), (0, 0), (0, 1), (1, 1), (1, 0)]
    return [(pos, phase) for pos, phase in rounds if sizes[pos] > 1 + phase]


def partner_of(sizes, pos, phase, here):
    there = list(here)
    near = here[pos] + (1 if (here[pos] + phase) % 2 == 0 else -1)
    if 0 <= near < sizes[pos]:
        there[pos] = near
    elif pos == 1:
        there[0] = here[0] ^ 1
    elif sizes[1] % 2:
        there[pos] = sizes[pos] - 1 - here[pos]
    else:
        there[1] = here[1] ^ 1
    return there


def swap_pairs(sizes, pos, phase):
    pairs = []
    for at_x in range(sizes[0]):
        for at_y in range(sizes[1]):
            for at_z in range(sizes[2]):
                there = partner_of(sizes, pos, phase, (at_x, at_y, at_z))
                if there != [at_x, at_y, at_z]:
                    pairs.append(
                        ((at_x * sizes[1] + at_y) * sizes[2] + at_z, (there[0] * sizes[1] + there[1]) * sizes[2] + there[2])
                    )
    return pairs


def has_neighbour(sizes, where, pos, phase):
    near = where[pos] + 1 - 2 * ((where[pos] + phase) & 1)
    return jnp.logical_and(near >= 0, near < sizes[pos])


def face_id(where, pos, phase):
    return 2 * pos + 1 - ((where[pos] + phase) & 1)


def join(left, right):
    return jnp.concatenate([left, right], axis=1)


def blocks(total):
    return [pl.ds(pos * (total // CHUNKS), total // CHUNKS) for pos in range(CHUNKS)]


def respond(response, straight, crossed, outgoing, part):
    outgoing[part, :] = (
        jnp.dot(response[0, part, :], straight[...], preferred_element_type=F32)
        + jnp.dot(response[1, part, :], crossed[...], preferred_element_type=F32)
    ).astype(BF16)


def pick_faces(picks, outgoing, outs):
    face = outs[0].shape[0]
    chosen = jnp.dot(picks[...], outgoing[...], preferred_element_type=F32).astype(BF16)
    for pos, out in enumerate(outs):
        out[...] = chosen[pos * face : (pos + 1) * face]


def add_traces(puts, arrived, source, values, part):
    traces = jnp.dot(puts[part, :], values[...], preferred_element_type=F32)
    return (traces + source[part, :].astype(F32)).astype(BF16)


def gather_values(arrived, values):
    face = arrived[0].shape[0]
    for pos, faces in enumerate(arrived):
        values[pl.ds(pos * face, face), :] = faces[...]


def turned(both):
    columns = both.shape[1] // 2
    return join(-both[:, columns:], both[:, :columns])


def first_kernel(sizes, rounds, linked_hbm, slots_hbm, source_hbm, response_hbm, *refs):
    count = len(rounds)
    outs = refs[:count]
    response, source, puts, picks = refs[count : count + 4]
    linked, slots, parts, crossed, outgoing, sems = refs[count + 4 :]
    unknowns, face = response.shape[1], slots.shape[2]
    small = [
        pltpu.make_async_copy(linked_hbm, linked, sems.at[0]),
        pltpu.make_async_copy(slots_hbm, slots, sems.at[1]),
        pltpu.make_async_copy(source_hbm, parts, sems.at[2]),
    ]
    large = [
        pltpu.make_async_copy(response_hbm.at[:, part, :], response.at[:, part, :], sems.at[3 + pos])
        for pos, part in enumerate(blocks(unknowns))
    ]
    for copy in small + large:
        copy.start()
    for copy in small:
        copy.wait()
    where = [lax.axis_index(axis) for axis in AXES]
    ids = [face_id(where, pos, phase) for pos, phase in rounds]
    rows = [slots[face_pos] for face_pos in ids]
    source[...] = join(parts[0], parts[1])
    crossed[...] = turned(source)
    upright = jnp.transpose(jnp.concatenate(rows + [rows[0]] * (-count % 8), axis=0))
    gates = [
        jnp.logical_and(linked[face_pos] != 0, has_neighbour(sizes, where, pos, phase))
        for face_pos, (pos, phase) in zip(ids, rounds)
    ]
    accepted = jnp.concatenate([jnp.where(gate, row, -1) for gate, row in zip(gates, rows)], axis=1)
    across = lax.broadcasted_iota(jnp.int32, (face, unknowns), 1)
    for pos in range(count):
        chosen = jnp.where(across == upright[:, pos : pos + 1], 1.0, 0.0)
        picks[pl.ds(pos * face, face), :] = chosen.astype(BF16)
    for part in blocks(unknowns):
        down = part.start + lax.broadcasted_iota(jnp.int32, (part.size, count * face), 0)
        puts[part, :] = jnp.where(down == accepted, 1.0, 0.0).astype(BF16)
    ready = 0
    for stage in STAGES:
        for copy in large[ready:stage]:
            copy.wait()
        for part in blocks(unknowns)[ready:stage]:
            respond(response, source, crossed, outgoing, part)
        ready = stage
    pick_faces(picks, outgoing, outs)


def sweep_kernel(count, response, source, puts, picks, *refs):
    arrived, outs = refs[:count], refs[count : 2 * count]
    values, straight, crossed, outgoing = refs[2 * count :]
    gather_values(arrived, values)
    for part in blocks(source.shape[0]):
        both = add_traces(puts, arrived, source, values, part)
        straight[part, :] = both
        crossed[part, :] = turned(both)
    for part in blocks(source.shape[0]):
        respond(response, straight, crossed, outgoing, part)
    pick_faces(picks, outgoing, outs)


def tint(at_x, at_y):
    return ((at_x >> 1) ^ (at_y >> 1)) & 1


def half_starts(sizes, half, eb, columns):
    chips = sizes[1] // 2
    return [(2 * pos + (half ^ tint(pos // chips, 2 * (pos % chips)))) * eb for pos in range(columns // (2 * eb))]


def columns_kernel(part, radiation, puts, out):
    out[...] = jnp.dot(radiation[part], puts[...], preferred_element_type=F32).astype(BF16)


def incident_kernel(radiation, source, puts, base, out):
    columns_kernel(1, radiation, puts, out)
    base[...] = jnp.dot(radiation[0], source[...], preferred_element_type=F32) + jnp.dot(
        radiation[1], turned(source[...]), preferred_element_type=F32
    )


def radiate_kernel(sizes, count, halves, eb, base, placed, placed_imag, *refs):
    arrived, outs = refs[:count], refs[count : count + 1 + halves]
    (values,) = refs[count + 1 + halves :]
    columns = base.shape[1] // 2
    gather_values(arrived, values)
    field = (
        base[...]
        + jnp.dot(placed[...], values[...], preferred_element_type=F32)
        + jnp.dot(placed_imag[...], turned(values[...]), preferred_element_type=F32)
    )
    along, across = lax.axis_index("gy"), lax.axis_index("gx")
    mine = (along & 1) ^ tint(across, along)
    for part in range(2):
        flat = jnp.transpose(field[:, part * columns : (part + 1) * columns])
        if not halves:
            outs[0][part] = flat
            continue
        split = [
            jnp.concatenate([flat[start : start + eb] for start in half_starts(sizes, half, eb, columns)], axis=0)
            for half in range(2)
        ]
        outs[0][part] = jnp.where(mine == 0, split[0], split[1])
        outs[1][part] = jnp.where(mine == 0, split[1], split[0])


def hbm_spec():
    return pl.BlockSpec(memory_space=pl.ANY)


def vmem_spec():
    return pl.BlockSpec(memory_space=pltpu.VMEM)


def in_hbm(value):
    return pltpu.with_memory_space_constraint(value, pltpu.HBM)


def in_vmem(value):
    return pltpu.with_memory_space_constraint(value, pltpu.VMEM)


def params():
    return pltpu.CompilerParams(vmem_limit_bytes=VMEM_LIMIT)


def first_sweep(sizes, rounds, linked, slots, source, response):
    unknowns, columns = source.shape[1:]
    face, count = slots.shape[2], len(rounds)
    kept = [
        (response.shape, BF16),
        ((unknowns, 2 * columns), BF16),
        ((unknowns, count * face), BF16),
        ((count * face, unknowns), BF16),
    ]
    outs = pl.pallas_call(
        functools.partial(first_kernel, sizes, rounds),
        out_shape=[jax.ShapeDtypeStruct((face, 2 * columns), BF16)] * count
        + [OUT_VMEM(shape, kind) for shape, kind in kept],
        in_specs=[hbm_spec()] * 4,
        out_specs=[vmem_spec()] * (count + len(kept)),
        scratch_shapes=[
            pltpu.SMEM(linked.shape, linked.dtype),
            pltpu.VMEM(slots.shape, slots.dtype),
            pltpu.VMEM(source.shape, BF16),
            pltpu.VMEM((unknowns, 2 * columns), BF16),
            pltpu.VMEM((unknowns, 2 * columns), BF16),
            pltpu.SemaphoreType.DMA((3 + CHUNKS,)),
        ],
        compiler_params=params(),
    )(in_hbm(linked), in_hbm(slots), in_hbm(source), in_hbm(response))
    return outs[:count], outs[count:]


def later_sweep(kept, arrived):
    response, source, puts, picks = kept
    count = len(arrived)
    return pl.pallas_call(
        functools.partial(sweep_kernel, count),
        out_shape=[jax.ShapeDtypeStruct(arrived[0].shape, BF16)] * count,
        in_specs=[vmem_spec()] * (4 + count),
        out_specs=[vmem_spec()] * count,
        scratch_shapes=[pltpu.VMEM((picks.shape[0], source.shape[1]), BF16)]
        + [pltpu.VMEM(source.shape, BF16)] * 3,
        compiler_params=params(),
    )(response, source, puts, picks, *arrived)


def cost(rows, depth, columns):
    moved = 2 * (rows * depth + depth * columns + rows * columns)
    return pl.CostEstimate(flops=2 * rows * depth * columns, bytes_accessed=moved, transcendentals=0)


def placed_real(radiation, puts):
    shape = (radiation.shape[1], puts.shape[1])
    return pl.pallas_call(
        functools.partial(columns_kernel, 0),
        out_shape=OUT_VMEM(shape, BF16),
        in_specs=[vmem_spec()] * 2,
        out_specs=vmem_spec(),
        cost_estimate=cost(shape[0], *puts.shape),
        compiler_params=params(),
    )(radiation, puts)


def placed_imag_and_incident(radiation, source, puts):
    angles = radiation.shape[1]
    return pl.pallas_call(
        incident_kernel,
        out_shape=[OUT_VMEM((angles, source.shape[1]), F32), OUT_VMEM((angles, puts.shape[1]), BF16)],
        in_specs=[vmem_spec()] * 3,
        out_specs=[vmem_spec()] * 2,
        cost_estimate=cost(2 * angles, *puts.shape),
        compiler_params=params(),
    )(radiation, source, puts)


def radiate(sizes, base, placed, placed_imag, arrived, halves, eb):
    columns = base.shape[1] // 2
    angles = base.shape[0]
    count = len(arrived)
    shape = (2, columns // 2 if halves else columns, angles)
    outs = [jax.ShapeDtypeStruct(shape, F32)] * (1 + int(halves))
    return pl.pallas_call(
        functools.partial(radiate_kernel, sizes, count, int(halves), eb),
        out_shape=outs,
        in_specs=[vmem_spec()] * (3 + count),
        out_specs=[vmem_spec()] * len(outs),
        scratch_shapes=[pltpu.VMEM((placed.shape[1], 2 * columns), BF16)],
        compiler_params=params(),
    )(base, placed, placed_imag, *arrived)


def bit_count(size):
    return size.bit_length() - 1


def mask_pairs(sizes, flips):
    pairs = []
    for at_x in range(sizes[0]):
        for at_y in range(sizes[1]):
            for at_z in range(sizes[2]):
                here = (at_x * sizes[1] + at_y) * sizes[2] + at_z
                there = ((at_x ^ flips[0]) * sizes[1] + (at_y ^ flips[1])) * sizes[2] + (at_z ^ flips[2])
                pairs.append((here, there))
    return pairs


def scatter_sum(parts, sizes, where, full):
    columns, angles = full
    bits = [bit_count(size) for size in sizes]
    halves = len(parts) > 1
    dims = {}
    shape = [2]
    for pos in (0, 1):
        for bit in reversed(range(bits[pos])):
            if halves and (pos, bit) == (1, 0):
                continue
            dims[(pos, bit)] = len(shape)
            shape.append(2)
    shape.append(columns // (sizes[0] * sizes[1]))
    for bit in reversed(range(bits[2])):
        dims[(2, bit)] = len(shape)
        shape.append(2)
    shape.append(angles // sizes[2])
    total = parts[0]
    if halves:
        total = total + lax.ppermute(parts[1], AXES, mask_pairs(sizes, (0, 1, 0)))
    total = total.reshape(shape)
    rest = sorted(item for item in dims if item[0] != 0) + sorted((item for item in dims if item[0] == 0), reverse=True)
    rounds = [rest[pos : pos + 2] for pos in range(0, len(rest), 2)]
    for order, group in enumerate(rounds):
        wide = order == len(rounds) - 1

        def taken(code):
            piece = total
            for place, (pos, bit) in enumerate(group):
                mine = (where[pos] >> bit) & 1
                piece = lax.dynamic_slice_in_dim(piece, mine ^ ((code >> place) & 1), 1, axis=dims[(pos, bit)])
            return piece

        got = []
        for code in reversed(range(1, 2 ** len(group))):
            flips = [0, 0, 0]
            for place, (pos, bit) in enumerate(group):
                flips[pos] |= ((code >> place) & 1) << bit
            if halves:
                flips[1] ^= tint(flips[0], flips[1])
            piece = taken(code) if wide else taken(code).astype(BF16)
            got.append(lax.ppermute(piece, AXES, mask_pairs(sizes, flips)))
        total = taken(0)
        for piece in got:
            total = total + piece.astype(F32)
    return total.reshape(2, columns // (sizes[0] * sizes[1]), angles // sizes[2])


def shards(sizes, incident, response, radiation, face_index, linked):
    source = incident[0, 0, 0]
    response_mat = response[0, 0, 0]
    radiation_mat = radiation[0, 0, 0]
    slots = face_index[0, 0, 0][:, None, :]
    where = [lax.axis_index(axis) for axis in AXES]
    rounds = swap_rounds(sizes)
    columns, angles = source.shape[2], radiation_mat.shape[1]
    faces, kept = first_sweep(sizes, rounds, linked[0, 0, 0], slots, source, response_mat)
    placed = placed_real(radiation_mat, kept[2])
    for turn in range(ITERS):
        if turn == ITERS - 1:
            source_now, puts_now, faces = lax.optimization_barrier((kept[1], kept[2], list(faces)))
            base, placed_imag = placed_imag_and_incident(radiation_mat, source_now, puts_now)
        arrived = [
            lax.ppermute(face, AXES, swap_pairs(sizes, pos, phase))
            for face, (pos, phase) in zip(faces, rounds)
        ]
        if turn == 0:
            placed, arrived = lax.optimization_barrier((placed, arrived))
        if turn < ITERS - 1:
            faces = later_sweep(kept, arrived)
    halves = sizes[1] % 2 == 0
    parts = radiate(sizes, base, placed, placed_imag, arrived, halves, columns // (sizes[0] * sizes[1]))
    return scatter_sum(parts, sizes, where, (columns, angles))


def solution(mesh):
    sizes = tuple(mesh.shape[axis] for axis in AXES)
    return jax.shard_map(
        functools.partial(shards, sizes),
        mesh=mesh,
        in_specs=(
            P("gx", "gy", "gz", None, None, None),
            P("gx", "gy", "gz", None, None, None),
            P("gx", "gy", "gz", None, None, None),
            P("gx", "gy", "gz", None, None),
            P("gx", "gy", "gz", None),
        ),
        out_specs=P(None, ("gx", "gy"), "gz"),
        check_vma=False,
    )
```
